32 devices in a mesh: gx: 8 (over z, x), gy: 4 (over y, core).
Axes of the slice: x: 2, y: 2, z: 4, core: 2. Of those that a mesh axis runs over, the one named last changes fastest.
Arguments:
- field: float32 [64, 32, 192], P('gx', 'gy'), may hold values from -6 to 6
- target: float32 [64, 32, 192], P('gx', 'gy'), may hold values from -6 to 6
- embed_weight: float32 [192, 256], replicated, may hold values from -0.4375 to 0.4375
- norm_gain: float32 [256], replicated, may hold values from 0.5 to 1.5
- attend_weight: float32 [256, 768], replicated, may hold values from -0.375 to 0.375
- output_weight: float32 [256, 256], replicated, may hold values from -0.375 to 0.375
- second_gain: float32 [256], replicated, may hold values from 0.5 to 1.5
- expand_weight: float32 [256, 512], replicated, may hold values from -0.375 to 0.375
- reduce_weight: float32 [512, 256], replicated, may hold values from -0.25 to 0.25
- decode_weight: float32 [256, 192], replicated, may hold values from -0.375 to 0.375
Outputs:
- loss: float32 [], replicated
- field_gradient: float32 [64, 32, 192], P('gx', 'gy')
- embed_gradient: float32 [192, 256], replicated
- norm_gradient: float32 [256], replicated
- attend_gradient: float32 [256, 768], replicated
- output_gradient: float32 [256, 256], replicated
- second_gradient: float32 [256], replicated
- expand_gradient: float32 [256, 512], replicated
- reduce_gradient: float32 [512, 256], replicated
- decode_gradient: float32 [256, 192], replicated
The draws below stay inside these ranges and needn't reach their ends.
All inputs are finite; a program needn't handle non-finite values.
Results may differ from the reference program's by a relative error of at most 0.0001.
Values sent between devices are 32-bit elements; how exact they have to be, the bound alone decides.
A program may use at most 128 MiB of HBM per device.

```python
import jax
import jax.numpy as jnp
from jax import lax

NZ = 64
PATCH = 4
D = 256
HEADS = 8
FF = 512
STEPS = 2
NX = 64
NY = 32
CELLS = 393216


def steps_of(key, dims, pieces, low, largest):
    level = 1.0
    for position, parts in pieces:
        heights = jax.random.uniform(jax.random.fold_in(jax.random.fold_in(key, 6), position), (parts,), jnp.float32, low / len(pieces), largest / len(pieces))
        level = level * jnp.repeat(jnp.exp(heights), dims[position] // parts).reshape((-1,) + (1,) * (len(dims) - 1 - position))
    return level


def bell_draw(rng, extent, scale, most, split=(), held_as=jnp.bfloat16):
    level = steps_of(rng, extent, split, -0.22, 0.18) if split else 1.0
    drawn = jax.random.normal(rng, extent, jnp.float32) * scale * level
    return jnp.minimum(jnp.maximum(drawn, -most), most).astype(held_as)


def setup_inputs(seed: int = 0) -> dict:
    arg_keys = jax.random.split(jax.random.key(seed), 11)
    field = bell_draw(arg_keys[0], (NX, NY, 3 * NZ), 1.0, 6.0, ((0, 8), (1, 4)), jnp.float32)
    target = bell_draw(arg_keys[1], (NX, NY, 3 * NZ), 1.0, 6.0, ((0, 8), (1, 4)), jnp.float32)
    embed_weight = bell_draw(arg_keys[2], (3 * PATCH * PATCH * PATCH, D), (3 * PATCH * PATCH * PATCH) ** -0.5, 0.4375, (), jnp.float32)
    norm_gain = jnp.clip(1.0 + 0.1 * jax.random.normal(arg_keys[3], (D,), jnp.float32), 0.5, 1.5)
    attend_weight = bell_draw(arg_keys[4], (D, 3 * D), D ** -0.5, 0.375, (), jnp.float32)
    output_weight = bell_draw(arg_keys[5], (D, D), D ** -0.5, 0.375, (), jnp.float32)
    second_gain = jnp.clip(1.0 + 0.1 * jax.random.normal(arg_keys[6], (D,), jnp.float32), 0.5, 1.5)
    expand_weight = bell_draw(arg_keys[7], (D, FF), D ** -0.5, 0.375, (), jnp.float32)
    reduce_weight = bell_draw(arg_keys[8], (FF, D), FF ** -0.5, 0.25, (), jnp.float32)
    decode_weight = bell_draw(arg_keys[9], (D, 3 * PATCH * PATCH * PATCH), D ** -0.5, 0.375, (), jnp.float32)
    return dict(field=field, target=target, embed_weight=embed_weight, norm_gain=norm_gain, attend_weight=attend_weight, output_weight=output_weight, second_gain=second_gain, expand_weight=expand_weight, reduce_weight=reduce_weight, decode_weight=decode_weight)


EXACT = lax.Precision.HIGHEST
EPSILON = 1e-06
TIME_STEP = 0.1
VISCOSITY = 0.5

def matmul(left, right):
    return jnp.dot(left, right, precision=EXACT)

def rms_scale(values, gain):
    power = lax.optimization_barrier(jnp.mean(values * values, axis=-1, keepdims=True))
    return values * lax.rsqrt(power + EPSILON) * gain

def closure(ext, params):
    embed_weight, norm_gain, attend_weight, output_weight, second_gain, expand_weight, reduce_weight, decode_weight = params
    wide, tall, depth = ext.shape
    levels = depth // 3
    across, along, upward = (wide // PATCH, tall // PATCH, levels // PATCH)
    patches = ext.reshape(across, PATCH, along, PATCH, 3, upward, PATCH).transpose(0, 2, 5, 4, 1, 3, 6)
    patches = patches.reshape(across, along, upward, 3 * PATCH * PATCH * PATCH)
    tokens = matmul(patches, embed_weight)
    width = tokens.shape[-1]
    head_size = width // HEADS
    mixed = matmul(rms_scale(tokens, norm_gain), attend_weight)
    inner_x, inner_y = (across - 2, along - 2)
    queries = mixed[1:-1, 1:-1, :, :width].reshape(inner_x, inner_y, upward, HEADS, head_size)
    keyset = mixed[:, :, :, width:2 * width]
    valset = mixed[:, :, :, 2 * width:]
    offsets = [(shift_x, shift_y) for shift_x in range(3) for shift_y in range(3)]
    keyblock = jnp.concatenate([keyset[sx:sx + inner_x, sy:sy + inner_y] for sx, sy in offsets], axis=2)
    valblock = jnp.concatenate([valset[sx:sx + inner_x, sy:sy + inner_y] for sx, sy in offsets], axis=2)
    keyblock = keyblock.reshape(inner_x, inner_y, 9 * upward, HEADS, head_size)
    valblock = valblock.reshape(inner_x, inner_y, 9 * upward, HEADS, head_size)
    factor = head_size ** (-0.5)
    scores = jnp.einsum('xyzhe,xywhe->xyhzw', queries, keyblock, precision=EXACT) * factor
    weights = jnp.exp(scores)
    weights = weights / lax.optimization_barrier(jnp.sum(weights, axis=-1, keepdims=True))
    attended = jnp.einsum('xyhzw,xywhe->xyzhe', weights, valblock, precision=EXACT)
    attended = attended.reshape(inner_x, inner_y, upward, width)
    middle = tokens[1:-1, 1:-1] + matmul(attended, output_weight)
    hidden = jax.nn.silu(matmul(rms_scale(middle, second_gain), expand_weight))
    middle = middle + matmul(hidden, reduce_weight)
    result = matmul(middle, decode_weight).reshape(inner_x, inner_y, upward, 3, PATCH, PATCH, PATCH)
    return result.transpose(0, 4, 1, 5, 3, 2, 6).reshape(inner_x * PATCH, inner_y * PATCH, depth)

def advance(ext, params):
    wide, tall, depth = ext.shape
    levels = depth // 3
    inner = ext[PATCH:wide - PATCH, PATCH:tall - PATCH]
    east = ext[PATCH + 1:wide - PATCH + 1, PATCH:tall - PATCH]
    west = ext[PATCH - 1:wide - PATCH - 1, PATCH:tall - PATCH]
    north = ext[PATCH:wide - PATCH, PATCH + 1:tall - PATCH + 1]
    south = ext[PATCH:wide - PATCH, PATCH - 1:tall - PATCH - 1]
    level = jnp.arange(depth, dtype=jnp.int32) % levels
    blank = jnp.zeros(inner.shape[:2] + (1,), jnp.float32)
    upper = jnp.where(level == levels - 1, 0.0, jnp.concatenate([inner[:, :, 1:], blank], axis=2))
    lower = jnp.where(level == 0, 0.0, jnp.concatenate([blank, inner[:, :, :-1]], axis=2))
    laplace = east + west + north + south + upper + lower - 6.0 * inner
    speed_x = jnp.concatenate([inner[:, :, 0:levels]] * 3, axis=2)
    speed_y = jnp.concatenate([inner[:, :, levels:2 * levels]] * 3, axis=2)
    speed_z = jnp.concatenate([inner[:, :, 2 * levels:]] * 3, axis=2)
    carried = 0.5 * (speed_x * (east - west) + speed_y * (north - south) + speed_z * (upper - lower))
    return inner + TIME_STEP * (VISCOSITY * laplace - carried + closure(ext, params))

def reference(field, target, embed_weight, norm_gain, attend_weight, output_weight, second_gain, expand_weight, reduce_weight, decode_weight):
    params = (embed_weight, norm_gain, attend_weight, output_weight, second_gain, expand_weight, reduce_weight, decode_weight)

    def misfit_of(start, weights):
        current = start
        for step in range(STEPS):
            padded = jnp.pad(current, ((PATCH, PATCH), (PATCH, PATCH), (0, 0)), mode='wrap')
            current = jax.checkpoint(advance)(padded, weights)
        residue = current - target
        return jnp.sum(residue * residue)
    misfit, pullback = jax.vjp(misfit_of, field, params)
    energy = jnp.sum(target * target)
    field_back, param_back = pullback(jnp.float32(1.0))
    scale = jnp.float32(CELLS) / energy
    loss = misfit / energy
    return (loss, scale * field_back, scale * param_back[0], scale * param_back[1], scale * param_back[2], scale * param_back[3], scale * param_back[4], scale * param_back[5], scale * param_back[6], scale * param_back[7])
```

```python
import functools

import jax
import jax.numpy as jnp
import numpy as np
from jax import lax
from jax.experimental import pallas as pl
from jax.experimental.pallas import tpu as pltpu
from jax.sharding import PartitionSpec as P

PATCH = 4
HEADS = 8
STEPS = 2

EPSILON = 1e-06
TIME_STEP = 0.1
VISCOSITY = 0.5
LANES = 128
MESH = pl.DeviceIdType.MESH
VMEM_LIMIT = 56 * 1024 * 1024
F32 = jnp.float32


def dot(left, right, dims):
    lh = left.astype(jnp.bfloat16)
    rh = right.astype(jnp.bfloat16)
    ll = (left - lh.astype(F32)).astype(jnp.bfloat16)
    rl = (right - rh.astype(F32)).astype(jnp.bfloat16)
    one = lambda a, b: lax.dot_general(a, b, (dims, ((), ())), preferred_element_type=F32)
    return one(lh, rh) + (one(lh, rl) + one(ll, rh))


def nn(a, b):
    return dot(a, b, ((1,), (0,)))


def nt(a, b):
    return dot(a, b, ((1,), (1,)))


def tn(a, b):
    return dot(a, b, ((0,), (0,)))


class Shape:
    def __init__(self, field_shape, width, hidden):
        wide, tall, depth = field_shape
        self.ax, self.ay, self.up = wide // PATCH, tall // PATCH, depth // 3 // PATCH
        self.ex, self.ey = self.ax + 2, self.ay + 2
        self.inner = self.ax * self.ay * self.up
        self.ext = self.ex * self.ey * self.up
        self.cube = PATCH**3
        self.feat = 4 * self.cube
        self.width, self.hidden = width, hidden

    def row(self, x, y):
        return (x * self.ey + y) * self.up

    def view(self, dx, dy):
        return [(self.row(x + 1 + dx, 1 + dy), self.ay * self.up) for x in range(self.ax)]

    def copies(self):
        out = []
        for dx in (-1, 0, 1):
            for dy in (-1, 0, 1):
                if dx == 0 and dy == 0:
                    continue
                xs = {1: [(self.ax - 1, 0)], -1: [(0, self.ex - 1)], 0: [(x, x + 1) for x in range(self.ax)]}[dx]
                ys = {1: (self.ay - 1, 0, 1), -1: (0, self.ey - 1, 1), 0: (0, 1, self.ay)}[dy]
                for src, dst in xs:
                    out.append(
                        (dx, dy, (src * self.ay + ys[0]) * self.up, self.row(dst, ys[1]), ys[2] * self.up)
                    )
        return out


def take(value, spans):
    return jnp.concatenate([value[s : s + n] for s, n in spans], axis=0)


def lroll(value, shift):
    return pltpu.roll(value, shift % value.shape[1], 1)


def iota(shape, dim):
    return lax.broadcasted_iota(jnp.int32, shape, dim)


def stencil_parts(sh, ext):
    shape = (sh.inner, sh.feat)
    lane = iota(shape, 1)
    px, py, pz = (lane // (PATCH * PATCH)) % PATCH, (lane // PATCH) % PATCH, lane % PATCH
    comp = lane // sh.cube
    level = iota(shape, 0) % sh.up
    u = take(ext, sh.view(0, 0))
    last = PATCH - 1

    def plus(here, there, pos, stride):
        return jnp.where(pos < last, lroll(here, -stride), lroll(there, last * stride))

    def minus(here, there, pos, stride):
        return jnp.where(pos > 0, lroll(here, stride), lroll(there, -last * stride))

    above = jnp.where(level == sh.up - 1, 0.0, pltpu.roll(u, sh.inner - 1, 0))
    below = jnp.where(level == 0, 0.0, pltpu.roll(u, 1, 0))
    sx, sy = PATCH * PATCH, PATCH
    east = plus(u, take(ext, sh.view(1, 0)), px, sx)
    west = minus(u, take(ext, sh.view(-1, 0)), px, sx)
    north = plus(u, take(ext, sh.view(0, 1)), py, sy)
    south = minus(u, take(ext, sh.view(0, -1)), py, sy)
    upper = plus(u, above, pz, 1)
    lower = minus(u, below, pz, 1)
    r1, r2, r3 = lroll(u, sh.cube), lroll(u, 2 * sh.cube), lroll(u, 3 * sh.cube)
    first, second = comp == 0, comp == 1
    vx = jnp.where(first, u, jnp.where(second, r1, r2))
    vy = jnp.where(first, r3, jnp.where(second, u, r1))
    vz = jnp.where(first, r2, jnp.where(second, r3, u))
    return u, (east, west, north, south, upper, lower), (vx, vy, vz), (px, py, pz, comp, level)


def stencil(sh, ext, closed):
    u, (east, west, north, south, upper, lower), (vx, vy, vz), _ = stencil_parts(sh, ext)
    laplace = east + west + north + south + upper + lower - 6.0 * u
    carried = 0.5 * (vx * (east - west) + vy * (north - south) + vz * (upper - lower))
    return u + TIME_STEP * (VISCOSITY * laplace - carried + closed)


def stencil_back(sh, ext, cot, out_ref):
    u, (east, west, north, south, upper, lower), (vx, vy, vz), where = stencil_parts(sh, ext)
    px, py, pz, comp, level = where
    g = TIME_STEP * cot
    total = cot - (6.0 * VISCOSITY) * g

    def summed(value):
        return (
            value
            + lroll(value, sh.cube)
            + lroll(value, 2 * sh.cube)
            + lroll(value, 3 * sh.cube)
        )

    fx = summed(-0.5 * g * (east - west))
    fy = summed(-0.5 * g * (north - south))
    fz = summed(-0.5 * g * (upper - lower))
    total += jnp.where(comp == 0, fx, jnp.where(comp == 1, fy, jnp.where(comp == 2, fz, 0.0)))
    last = PATCH - 1

    def sides(pos, stride, speed):
        high = g * (VISCOSITY - 0.5 * speed)
        low = g * (VISCOSITY + 0.5 * speed)
        here = lroll(jnp.where(pos < last, high, 0.0), stride) + lroll(jnp.where(pos > 0, low, 0.0), -stride)
        after = lroll(jnp.where(pos == last, high, 0.0), -last * stride)
        before = lroll(jnp.where(pos == 0, low, 0.0), last * stride)
        return here, after, before

    here, east_back, west_back = sides(px, PATCH * PATCH, vx)
    total += here
    here, north_back, south_back = sides(py, PATCH, vy)
    total += here
    here, above_back, below_back = sides(pz, 1, vz)
    total += here
    total += jnp.where(level == 0, 0.0, pltpu.roll(above_back, 1, 0))
    total += jnp.where(level == sh.up - 1, 0.0, pltpu.roll(below_back, sh.inner - 1, 0))
    for value, shift in (
        (total, (0, 0)),
        (east_back, (1, 0)),
        (west_back, (-1, 0)),
        (north_back, (0, 1)),
        (south_back, (0, -1)),
    ):
        at = 0
        for s, n in sh.view(*shift):
            out_ref[s : s + n, :] += value[at : at + n]
            at += n


def head_split(sh, value):
    head = iota(value.shape, 1) // (sh.width // HEADS)
    return jnp.concatenate([jnp.where(head == h, value, 0.0) for h in range(HEADS)], axis=0)


def head_join(sh, value):
    head = iota((sh.inner, sh.width), 1) // (sh.width // HEADS)
    total = jnp.zeros((sh.inner, sh.width), F32)
    for h in range(HEADS):
        total = jnp.where(head == h, value[h * sh.inner : (h + 1) * sh.inner], total)
    return total


def inverse_rms(value):
    return lax.rsqrt(jnp.mean(value * value, axis=-1, keepdims=True) + EPSILON)


def forward(sh, ext, w):
    we, g1, wa, wo, g2, wx, wr, wd = w
    d = sh.width
    tokens = nn(ext, we[...])
    normed = tokens * inverse_rms(tokens) * g1[...]
    queries = nn(take(normed, sh.view(0, 0)), wa[:, :d])
    mixed = nn(normed, wa[:, d:])
    keys, values = mixed[:, :d], mixed[:, d:]
    shape = (HEADS * sh.inner, sh.ext)
    qcol = (iota(shape, 0) % sh.inner) // sh.up
    kcol = iota(shape, 1) // sh.up
    dx = kcol // sh.ey - qcol // sh.ay
    dy = kcol % sh.ey - qcol % sh.ay
    seen = (dx >= 0) & (dx <= 2) & (dy >= 0) & (dy <= 2)
    scores = nt(head_split(sh, queries), keys) * ((d // HEADS) ** -0.5)
    weights = jnp.exp(jnp.where(seen, scores, -1e30))
    weights = weights / jnp.sum(weights, axis=-1, keepdims=True)
    attended = head_join(sh, nn(weights, values))
    mid = take(tokens, sh.view(0, 0)) + nn(attended, wo[...])
    pre = nn(mid * inverse_rms(mid) * g2[...], wx[...])
    late = mid + nn(pre / (1.0 + jnp.exp(-pre)), wr[...])
    return nn(late, wd[...]), (tokens, queries, keys, values, weights, attended, mid, pre, late)


def backward(sh, ext, w, saved, cot, back_ref, emit):
    we, g1, wa, wo, g2, wx, wr, wd = w
    d = sh.width
    tokens, queries, keys, values, weights, attended, mid, pre, late = saved
    dclosed = TIME_STEP * cot
    emit("decode", tn(late, dclosed))
    dlate = nt(dclosed, wd[...])
    sig = 1.0 / (1.0 + jnp.exp(-pre))
    emit("reduce", tn(pre * sig, dlate))
    dpre = nt(dlate, wr[...]) * (sig * (1.0 + pre * (1.0 - sig)))
    r2 = inverse_rms(mid)
    unit = mid * r2
    emit("expand", tn(unit * g2[...], dpre))
    dn = nt(dpre, wx[...])
    emit("second", jnp.sum(dn * unit, axis=0, keepdims=True))
    y = dn * g2[...]
    dmid = dlate + r2 * (y - unit * jnp.mean(y * unit, axis=-1, keepdims=True))
    emit("output", tn(attended, dmid))
    dsplit = head_split(sh, nt(dmid, wo[...]))
    dweights = nt(dsplit, values)
    dvalues = tn(weights, dsplit)
    dscores = weights * (dweights - jnp.sum(dweights * weights, axis=-1, keepdims=True))
    dscores = dscores * ((d // HEADS) ** -0.5)
    dqueries = head_join(sh, nn(dscores, keys))
    dkeys = tn(dscores, head_split(sh, queries))
    r1 = inverse_rms(tokens)
    unit = tokens * r1
    normed = unit * g1[...]
    emit("query", tn(take(normed, sh.view(0, 0)), dqueries))
    emit("key", tn(normed, dkeys))
    emit("value", tn(normed, dvalues))
    dn = nt(dkeys, wa[:, d : 2 * d]) + nt(dvalues, wa[:, 2 * d :])
    dinner = nt(dqueries, wa[:, :d])
    back_ref[...] = dn
    at = 0
    for s, n in sh.view(0, 0):
        back_ref[s : s + n, :] += dinner[at : at + n]
        at += n
    dn = back_ref[...]
    emit("norm", jnp.sum(dn * unit, axis=0, keepdims=True))
    y = dn * g1[...]
    back_ref[...] = r1 * (y - unit * jnp.mean(y * unit, axis=-1, keepdims=True))
    at = 0
    for s, n in sh.view(0, 0):
        back_ref[s : s + n, :] += dmid[at : at + n]
        at += n
    dtokens = back_ref[...]
    emit("embed", tn(ext, dtokens))
    back_ref[...] = nt(dtokens, we[...])
    stencil_back(sh, ext, cot, back_ref)


class Packing:
    def __init__(self, sh, devices):
        d = sh.width
        sizes = [
            ("reduce", sh.hidden),
            ("expand", d * (sh.hidden // d)),
            ("decode", d),
            ("output", d),
            ("query", d),
            ("key", d),
            ("value", d),
            ("embed", sh.feat - sh.cube),
            ("small", 8),
        ]
        self.at, row = {}, 0
        for name, n in sizes:
            self.at[name] = (row, n)
            row += n
        unit = 8 * devices
        self.rows = -(-row // unit) * unit
        self.used = row
        self.unit = unit


SMALL = {"norm": 0, "second": 1, "misfit": 2, "energy": 3}


def make_emit(sh, pk, out_ref, prior):
    def emit(name, value):
        if name in SMALL:
            r = pk.at["small"][0] + SMALL[name]
            value = value if prior is None else value + prior[r : r + 1, :]
            out_ref[r : r + 1, :] = value
            return
        row, n = pk.at[name]
        if name == "embed":
            value = value[:n]
        pieces = [value]
        if name == "expand":
            pieces = [value[:, k : k + sh.width] for k in range(0, sh.hidden, sh.width)]
        for piece in pieces:
            m = piece.shape[0]
            add = piece if prior is None else piece + prior[row : row + m, :]
            out_ref[row : row + m, :] = add
            row += m

    return emit


def first_kernel(sh, *refs):
    ext, w, (new, *saved) = refs[0], refs[1:9], refs[9:]
    e = ext[...]
    closed, kept = forward(sh, e, w)
    new[...] = stencil(sh, e, closed)
    for ref, value in zip(saved, kept):
        ref[...] = value


def middle_kernel(sh, pk, *refs):
    ext, target, w, (back, packed) = refs[0], refs[1], refs[2:10], refs[10:12]
    packed[pk.at["small"][0] :, :] = jnp.zeros((pk.rows - pk.at["small"][0], sh.width), F32)
    emit = make_emit(sh, pk, packed, None)
    e = ext[...]
    closed, kept = forward(sh, e, w)
    goal = target[...]
    residue = stencil(sh, e, closed) - goal
    emit("misfit", jnp.sum(residue * residue, axis=0, keepdims=True))
    emit("energy", jnp.sum(goal * goal, axis=0, keepdims=True))
    backward(sh, e, w, kept, 2.0 * residue, back, emit)


def last_kernel(sh, pk, *refs):
    ext, cot, w, saved, prior, (back, packed) = refs[0], refs[1], refs[2:10], refs[10:19], refs[19], refs[20:22]
    packed[pk.at["small"][0] :, :] = prior[pk.at["small"][0] :, :]
    emit = make_emit(sh, pk, packed, prior)
    kept = tuple(ref[...] for ref in saved)
    backward(sh, ext[...], w, kept, cot[...], back, emit)


def neighbour(counts, dx, dy):
    nx, ny = counts
    return (
        lax.rem(lax.axis_index("gx") + (dx + nx), nx),
        lax.rem(lax.axis_index("gy") + (dy + ny), ny),
    )


def greet(devices):
    barrier = pltpu.get_barrier_semaphore()
    for device in devices:
        pl.semaphore_signal(barrier, inc=1, device_id=device, device_id_type=MESH)
    pl.semaphore_wait(barrier, len(devices))


AROUND = [(dx, dy) for dx in (-1, 0, 1) for dy in (-1, 0, 1) if (dx, dy) != (0, 0)]


def spread_kernel(sh, counts, u, ext, send, recv):
    greet([neighbour(counts, dx, dy) for dx, dy in AROUND])
    started = []
    for i, (dx, dy, src, dst, n) in enumerate(sh.copies()):
        copy = pltpu.make_async_remote_copy(
            src_ref=u.at[pl.ds(src, n)],
            dst_ref=ext.at[pl.ds(dst, n)],
            send_sem=send.at[i],
            recv_sem=recv.at[i],
            device_id=neighbour(counts, dx, dy),
            device_id_type=MESH,
        )
        copy.start()
        started.append(copy)
    at = 0
    for s, n in sh.view(0, 0):
        ext[s : s + n, :] = u[at : at + n, :]
        at += n
    for copy in started:
        copy.wait()


def gather_kernel(sh, counts, back, out, slots, send, recv):
    greet([neighbour(counts, dx, dy) for dx, dy in AROUND])
    started = []
    place = 0
    for i, (dx, dy, dst, src, n) in enumerate(sh.copies()):
        copy = pltpu.make_async_remote_copy(
            src_ref=back.at[pl.ds(src, n)],
            dst_ref=slots.at[pl.ds(place, n)],
            send_sem=send.at[i],
            recv_sem=recv.at[i],
            device_id=neighbour(counts, -dx, -dy),
            device_id_type=MESH,
        )
        copy.start()
        started.append((copy, dst, place, n))
        place += n
    at = 0
    for s, n in sh.view(0, 0):
        out[at : at + n, :] = back[s : s + n, :]
        at += n
    for copy, dst, place, n in started:
        copy.wait()
        out[dst : dst + n, :] += slots[place : place + n, :]


def exchange_orders(counts):
    nx, ny = counts
    bits = lambda n: [1 << k for k in range(n.bit_length() - 1)]
    ys = [("gy", s) for s in bits(ny)]
    xs = [("gx", s) for s in bits(nx)]
    head, y, x, z = ys[:1], ys[1:], xs[:1], xs[1:]
    return [head + y + x + z, head + x + z + y, head + z + y + x]


def partner(axis, s):
    gx, gy = lax.axis_index("gx"), lax.axis_index("gy")
    index = gx if axis == "gx" else gy
    bit = lax.rem(index // s, 2)
    other = index + s - 2 * s * bit
    return bit, ((other, gy) if axis == "gx" else (gx, other))


def reduce_kernel(counts, parts, packed, out, acc, slots, send, recv):
    orders = exchange_orders(counts)
    greet([partner(*step)[1] for step in orders[0]])
    steps = len(orders[0])
    where = []
    base = 0
    for start, rows in parts:
        where.append([start, rows, base])
        base += rows
    source = packed
    history = [[] for _ in parts]
    for k in range(steps):
        flight = []
        for p, (start, rows, base) in enumerate(where):
            bit, device = partner(*orders[p][k])
            half = rows // 2
            keep = pl.multiple_of(start + bit * half, 8)
            give = pl.multiple_of(start + half - bit * half, 8)
            copy = pltpu.make_async_remote_copy(
                src_ref=source.at[pl.ds(give, half)],
                dst_ref=slots.at[pl.ds(base, half)],
                send_sem=send.at[p, k],
                recv_sem=recv.at[p, k],
                device_id=device,
                device_id_type=MESH,
            )
            copy.start()
            flight.append((copy, keep, half, base))
            history[p].append((keep, half, device))
        for p, (copy, keep, half, base) in enumerate(flight):
            copy.wait()
            target = acc if k < steps - 1 else out
            target[pl.ds(keep, half), :] = source[pl.ds(keep, half), :] + slots[pl.ds(base, half), :]
            where[p] = [keep, half, base + half]
        source = acc
    for k in reversed(range(steps)):
        flight = []
        for p in range(len(parts)):
            keep, half, device = history[p][k]
            copy = pltpu.make_async_remote_copy(
                src_ref=out.at[pl.ds(keep, half)],
                dst_ref=out.at[pl.ds(keep, half)],
                send_sem=send.at[p, steps + k],
                recv_sem=recv.at[p, steps + k],
                device_id=device,
                device_id_type=MESH,
            )
            copy.start()
            flight.append(copy)
        for copy in flight:
            copy.wait()


def finish_kernel(sh, pk, entries, packed, cot, loss, field, embed, norm, attend, output, second, expand, reduce, decode):
    small = pk.at["small"][0]
    energy = jnp.sum(packed[small + SMALL["energy"] : small + SMALL["energy"] + 1, :], axis=1, keepdims=True)
    misfit = jnp.sum(packed[small + SMALL["misfit"] : small + SMALL["misfit"] + 1, :], axis=1, keepdims=True)
    scale = entries / energy
    loss[...] = misfit / energy
    field[...] = scale * cot[...]
    norm[...] = scale * packed[small : small + 1, :]
    second[...] = scale * packed[small + 1 : small + 2, :]

    def piece(name):
        row, n = pk.at[name]
        return scale * packed[row : row + n, :]

    embed[...] = piece("embed")
    output[...] = piece("output")
    reduce[...] = piece("reduce")
    decode[...] = piece("decode")[:, : decode.shape[1]]
    d = sh.width
    for k, name in enumerate(("query", "key", "value")):
        attend[:, k * d : (k + 1) * d] = piece(name)
    row = pk.at["expand"][0]
    for k in range(sh.hidden // d):
        expand[:, k * d : (k + 1) * d] = scale * packed[row + k * d : row + (k + 1) * d, :]


def call(kernel, outs, args, scratch=(), collective=None):
    vm = pl.BlockSpec(memory_space=pltpu.VMEM)
    extra = {} if collective is None else dict(collective_id=collective, has_side_effects=True)
    return pl.pallas_call(
        kernel,
        out_shape=[jax.ShapeDtypeStruct(s, F32) for s in outs],
        in_specs=[vm] * len(args),
        out_specs=[vm] * len(outs),
        scratch_shapes=list(scratch),
        compiler_params=pltpu.CompilerParams(vmem_limit_bytes=VMEM_LIMIT, **extra),
    )(*args)


def to_tokens(sh, block):
    x = block.reshape(sh.ax, PATCH, sh.ay, PATCH, 3, sh.up, PATCH).transpose(0, 2, 5, 4, 1, 3, 6)
    return jnp.pad(x.reshape(sh.inner, 3 * sh.cube), ((0, 0), (0, sh.cube)))


def from_tokens(sh, tokens, shape):
    x = tokens[:, : 3 * sh.cube].reshape(sh.ax, sh.ay, sh.up, 3, PATCH, PATCH, PATCH)
    return x.transpose(0, 4, 1, 5, 3, 2, 6).reshape(shape)


def shards(counts, field, target, embed_weight, norm_gain, attend_weight, output_weight, second_gain, expand_weight, reduce_weight, decode_weight):
    width, hidden = expand_weight.shape
    sh = Shape(field.shape, width, hidden)
    devices = counts[0] * counts[1]
    pk = Packing(sh, devices)
    blocks = pk.rows // pk.unit
    cuts = [blocks * k // 3 for k in range(4)]
    parts = [(a * pk.unit, (b - a) * pk.unit) for a, b in zip(cuts, cuts[1:]) if b > a]
    weights = (
        jnp.pad(embed_weight, ((0, sh.cube), (0, 0))),
        norm_gain.reshape(1, width),
        attend_weight,
        output_weight,
        second_gain.reshape(1, width),
        expand_weight,
        reduce_weight,
        jnp.pad(decode_weight, ((0, 0), (0, sh.cube))),
    )
    ext_shape, inner_shape = (sh.ext, sh.feat), (sh.inner, sh.feat)
    slabs = sh.copies()
    sems = [pltpu.SemaphoreType.DMA((len(slabs),))] * 2
    slot_rows = sum(s[4] for s in slabs)

    def spread(u):
        return call(functools.partial(spread_kernel, sh, counts), [ext_shape], (u,), sems, 1)[0]

    def gather(back):
        scratch = [pltpu.VMEM((slot_rows, sh.feat), F32)] + sems
        return call(functools.partial(gather_kernel, sh, counts), [inner_shape], (back,), scratch, 2)[0]

    tokens_shape, query_shape = (sh.ext, width), (sh.inner, width)
    saved_shapes = [
        tokens_shape,
        query_shape,
        tokens_shape,
        tokens_shape,
        (HEADS * sh.inner, sh.ext),
        query_shape,
        query_shape,
        (sh.inner, hidden),
        query_shape,
    ]
    goal = to_tokens(sh, target)
    ext0 = spread(to_tokens(sh, field))
    new, *saved = call(functools.partial(first_kernel, sh), [inner_shape] + saved_shapes, (ext0,) + weights)
    ext1 = spread(new)
    packed_shape = (pk.rows, width)
    back, packed = call(functools.partial(middle_kernel, sh, pk), [ext_shape, packed_shape], (ext1, goal) + weights)
    cot = gather(back)
    back, packed = call(
        functools.partial(last_kernel, sh, pk),
        [ext_shape, packed_shape],
        (ext0, cot) + weights + tuple(saved) + (packed,),
    )
    cot = gather(back)
    steps = len(exchange_orders(counts)[0])
    summed = call(
        functools.partial(reduce_kernel, counts, parts),
        [packed_shape],
        (packed,),
        [
            pltpu.VMEM(packed_shape, F32),
            pltpu.VMEM(packed_shape, F32),
            pltpu.SemaphoreType.DMA((len(parts), 2 * steps)),
            pltpu.SemaphoreType.DMA((len(parts), 2 * steps)),
        ],
        3,
    )[0]
    entries = float(np.prod(field.shape) * devices)
    params = (embed_weight, norm_gain, attend_weight, output_weight, second_gain, expand_weight, reduce_weight, decode_weight)
    outs = [(1, 1), inner_shape] + [p.shape if p.ndim == 2 else (1, width) for p in params]
    done = call(functools.partial(finish_kernel, sh, pk, entries), outs, (summed, cot))
    grads = tuple(g.reshape(p.shape) for g, p in zip(done[2:], params))
    return (done[0].reshape(()), from_tokens(sh, done[1], field.shape)) + grads


def solution(mesh):
    counts = (mesh.shape["gx"], mesh.shape["gy"])
    in_specs = (P("gx", "gy", None), P("gx", "gy", None), P(), P(), P(), P(), P(), P(), P(), P())
    out_specs = (P(), P("gx", "gy", None), P(), P(), P(), P(), P(), P(), P(), P())
    return jax.shard_map(
        functools.partial(shards, counts), mesh=mesh, in_specs=in_specs, out_specs=out_specs, check_vma=False
    )
```

```python
import functools

import jax
import jax.numpy as jnp
import numpy as np
from jax import lax
from jax.experimental import pallas as pl
from jax.experimental.pallas import tpu as pltpu
from jax.sharding import PartitionSpec as P

PATCH = 4
HEADS = 8
STEPS = 2

EPSILON = 1e-06
TIME_STEP = 0.1
VISCOSITY = 0.5
LANES = 128
MESH = pl.DeviceIdType.MESH
VMEM_LIMIT = 56 * 1024 * 1024
F32 = jnp.float32


def dot(left, right, dims):
    lh = left.astype(jnp.bfloat16)
    rh = right.astype(jnp.bfloat16)
    ll = (left - lh.astype(F32)).astype(jnp.bfloat16)
    rl = (right - rh.astype(F32)).astype(jnp.bfloat16)
    one = lambda a, b: lax.dot_general(a, b, (dims, ((), ())), preferred_element_type=F32)
    return one(lh, rh) + (one(lh, rl) + one(ll, rh))


def nn(a, b):
    return dot(a, b, ((1,), (0,)))


def nt(a, b):
    return dot(a, b, ((1,), (1,)))


def tn(a, b):
    return dot(a, b, ((0,), (0,)))


class Shape:
    def __init__(self, field_shape, width, hidden):
        wide, tall, depth = field_shape
        self.ax, self.ay, self.up = wide // PATCH, tall // PATCH, depth // 3 // PATCH
        self.ex, self.ey = self.ax + 2, self.ay + 2
        self.inner = self.ax * self.ay * self.up
        self.ext = self.ex * self.ey * self.up
        self.cube = PATCH**3
        self.feat = 4 * self.cube
        self.width, self.hidden = width, hidden

    def row(self, x, y):
        return (x * self.ey + y) * self.up

    def view(self, dx, dy):
        return [(self.row(x + 1 + dx, 1 + dy), self.ay * self.up) for x in range(self.ax)]

    def copies(self):
        out = []
        for dx in (-1, 0, 1):
            for dy in (-1, 0, 1):
                if dx == 0 and dy == 0:
                    continue
                xs = {1: [(self.ax - 1, 0)], -1: [(0, self.ex - 1)], 0: [(x, x + 1) for x in range(self.ax)]}[dx]
                ys = {1: (self.ay - 1, 0, 1), -1: (0, self.ey - 1, 1), 0: (0, 1, self.ay)}[dy]
                for src, dst in xs:
                    out.append(
                        (dx, dy, (src * self.ay + ys[0]) * self.up, self.row(dst, ys[1]), ys[2] * self.up)
                    )
        return out


def take(value, spans):
    return jnp.concatenate([value[s : s + n] for s, n in spans], axis=0)


def lroll(value, shift):
    return pltpu.roll(value, shift % value.shape[1], 1)


def iota(shape, dim):
    return lax.broadcasted_iota(jnp.int32, shape, dim)


def stencil_parts(sh, ext):
    shape = (sh.inner, sh.feat)
    lane = iota(shape, 1)
    px, py, pz = (lane // (PATCH * PATCH)) % PATCH, (lane // PATCH) % PATCH, lane % PATCH
    comp = lane // sh.cube
    level = iota(shape, 0) % sh.up
    u = take(ext, sh.view(0, 0))
    last = PATCH - 1

    def plus(here, there, pos, stride):
        return jnp.where(pos < last, lroll(here, -stride), lroll(there, last * stride))

    def minus(here, there, pos, stride):
        return jnp.where(pos > 0, lroll(here, stride), lroll(there, -last * stride))

    above = jnp.where(level == sh.up - 1, 0.0, pltpu.roll(u, sh.inner - 1, 0))
    below = jnp.where(level == 0, 0.0, pltpu.roll(u, 1, 0))
    sx, sy = PATCH * PATCH, PATCH
    east = plus(u, take(ext, sh.view(1, 0)), px, sx)
    west = minus(u, take(ext, sh.view(-1, 0)), px, sx)
    north = plus(u, take(ext, sh.view(0, 1)), py, sy)
    south = minus(u, take(ext, sh.view(0, -1)), py, sy)
    upper = plus(u, above, pz, 1)
    lower = minus(u, below, pz, 1)
    r1, r2, r3 = lroll(u, sh.cube), lroll(u, 2 * sh.cube), lroll(u, 3 * sh.cube)
    first, second = comp == 0, comp == 1
    vx = jnp.where(first, u, jnp.where(second, r1, r2))
    vy = jnp.where(first, r3, jnp.where(second, u, r1))
    vz = jnp.where(first, r2, jnp.where(second, r3, u))
    return u, (east, west, north, south, upper, lower), (vx, vy, vz), (px, py, pz, comp, level)


def stencil(sh, ext, closed):
    u, (east, west, north, south, upper, lower), (vx, vy, vz), _ = stencil_parts(sh, ext)
    laplace = east + west + north + south + upper + lower - 6.0 * u
    carried = 0.5 * (vx * (east - west) + vy * (north - south) + vz * (upper - lower))
    return u + TIME_STEP * (VISCOSITY * laplace - carried + closed)


def stencil_back(sh, ext, cot, out_ref):
    u, (east, west, north, south, upper, lower), (vx, vy, vz), where = stencil_parts(sh, ext)
    px, py, pz, comp, level = where
    g = TIME_STEP * cot
    total = cot - (6.0 * VISCOSITY) * g

    def summed(value):
        return (
            value
            + lroll(value, sh.cube)
            + lroll(value, 2 * sh.cube)
            + lroll(value, 3 * sh.cube)
        )

    fx = summed(-0.5 * g * (east - west))
    fy = summed(-0.5 * g * (north - south))
    fz = summed(-0.5 * g * (upper - lower))
    total += jnp.where(comp == 0, fx, jnp.where(comp == 1, fy, jnp.where(comp == 2, fz, 0.0)))
    last = PATCH - 1

    def sides(pos, stride, speed):
        high = g * (VISCOSITY - 0.5 * speed)
        low = g * (VISCOSITY + 0.5 * speed)
        here = lroll(jnp.where(pos < last, high, 0.0), stride) + lroll(jnp.where(pos > 0, low, 0.0), -stride)
        after = lroll(jnp.where(pos == last, high, 0.0), -last * stride)
        before = lroll(jnp.where(pos == 0, low, 0.0), last * stride)
        return here, after, before

    here, east_back, west_back = sides(px, PATCH * PATCH, vx)
    total += here
    here, north_back, south_back = sides(py, PATCH, vy)
    total += here
    here, above_back, below_back = sides(pz, 1, vz)
    total += here
    total += jnp.where(level == 0, 0.0, pltpu.roll(above_back, 1, 0))
    total += jnp.where(level == sh.up - 1, 0.0, pltpu.roll(below_back, sh.inner - 1, 0))
    for value, shift in (
        (total, (0, 0)),
        (east_back, (1, 0)),
        (west_back, (-1, 0)),
        (north_back, (0, 1)),
        (south_back, (0, -1)),
    ):
        at = 0
        for s, n in sh.view(*shift):
            out_ref[s : s + n, :] += value[at : at + n]
            at += n


def head_split(sh, value):
    head = iota(value.shape, 1) // (sh.width // HEADS)
    return jnp.concatenate([jnp.where(head == h, value, 0.0) for h in range(HEADS)], axis=0)


def head_join(sh, value):
    head = iota((sh.inner, sh.width), 1) // (sh.width // HEADS)
    total = jnp.zeros((sh.inner, sh.width), F32)
    for h in range(HEADS):
        total = jnp.where(head == h, value[h * sh.inner : (h + 1) * sh.inner], total)
    return total


def inverse_rms(value):
    return lax.rsqrt(jnp.mean(value * value, axis=-1, keepdims=True) + EPSILON)


def forward(sh, ext, w):
    we, g1, wa, wo, g2, wx, wr, wd = w
    d = sh.width
    tokens = nn(ext, we[...])
    normed = tokens * inverse_rms(tokens) * g1[...]
    queries = nn(take(normed, sh.view(0, 0)), wa[:, :d])
    mixed = nn(normed, wa[:, d:])
    keys, values = mixed[:, :d], mixed[:, d:]
    shape = (HEADS * sh.inner, sh.ext)
    qcol = (iota(shape, 0) % sh.inner) // sh.up
    kcol = iota(shape, 1) // sh.up
    dx = kcol // sh.ey - qcol // sh.ay
    dy = kcol % sh.ey - qcol % sh.ay
    seen = (dx >= 0) & (dx <= 2) & (dy >= 0) & (dy <= 2)
    scores = nt(head_split(sh, queries), keys) * ((d // HEADS) ** -0.5)
    weights = jnp.exp(jnp.where(seen, scores, -1e30))
    weights = weights / jnp.sum(weights, axis=-1, keepdims=True)
    attended = head_join(sh, nn(weights, values))
    mid = take(tokens, sh.view(0, 0)) + nn(attended, wo[...])
    pre = nn(mid * inverse_rms(mid) * g2[...], wx[...])
    late = mid + nn(pre / (1.0 + jnp.exp(-pre)), wr[...])
    return nn(late, wd[...]), (tokens, queries, keys, values, weights, attended, mid, pre, late)


def backward(sh, ext, w, saved, cot, back_ref, emit):
    we, g1, wa, wo, g2, wx, wr, wd = w
    d = sh.width
    tokens, queries, keys, values, weights, attended, mid, pre, late = saved
    dclosed = TIME_STEP * cot
    emit("decode", tn(late, dclosed))
    dlate = nt(dclosed, wd[...])
    sig = 1.0 / (1.0 + jnp.exp(-pre))
    emit("reduce", tn(pre * sig, dlate))
    dpre = nt(dlate, wr[...]) * (sig * (1.0 + pre * (1.0 - sig)))
    r2 = inverse_rms(mid)
    unit = mid * r2
    emit("expand", tn(unit * g2[...], dpre))
    dn = nt(dpre, wx[...])
    emit("second", jnp.sum(dn * unit, axis=0, keepdims=True))
    y = dn * g2[...]
    dmid = dlate + r2 * (y - unit * jnp.mean(y * unit, axis=-1, keepdims=True))
    emit("output", tn(attended, dmid))
    dsplit = head_split(sh, nt(dmid, wo[...]))
    dweights = nt(dsplit, values)
    dvalues = tn(weights, dsplit)
    dscores = weights * (dweights - jnp.sum(dweights * weights, axis=-1, keepdims=True))
    dscores = dscores * ((d // HEADS) ** -0.5)
    dqueries = head_join(sh, nn(dscores, keys))
    dkeys = tn(dscores, head_split(sh, queries))
    r1 = inverse_rms(tokens)
    unit = tokens * r1
    normed = unit * g1[...]
    emit("query", tn(take(normed, sh.view(0, 0)), dqueries))
    emit("key", tn(normed, dkeys))
    emit("value", tn(normed, dvalues))
    dn = nt(dkeys, wa[:, d : 2 * d]) + nt(dvalues, wa[:, 2 * d :])
    dinner = nt(dqueries, wa[:, :d])
    back_ref[...] = dn
    at = 0
    for s, n in sh.view(0, 0):
        back_ref[s : s + n, :] += dinner[at : at + n]
        at += n
    dn = back_ref[...]
    emit("norm", jnp.sum(dn * unit, axis=0, keepdims=True))
    y = dn * g1[...]
    back_ref[...] = r1 * (y - unit * jnp.mean(y * unit, axis=-1, keepdims=True))
    at = 0
    for s, n in sh.view(0, 0):
        back_ref[s : s + n, :] += dmid[at : at + n]
        at += n
    dtokens = back_ref[...]
    emit("embed", tn(ext, dtokens))
    back_ref[...] = nt(dtokens, we[...])
    stencil_back(sh, ext, cot, back_ref)


class Packing:
    def __init__(self, sh, devices):
        d = sh.width
        sizes = [
            ("reduce", sh.hidden),
            ("expand", d * (sh.hidden // d)),
            ("decode", d),
            ("output", d),
            ("query", d),
            ("key", d),
            ("value", d),
            ("embed", sh.feat - sh.cube),
            ("small", 8),
        ]
        self.at, row = {}, 0
        for name, n in sizes:
            self.at[name] = (row, n)
            row += n
        unit = 8 * devices
        self.rows = -(-row // unit) * unit
        self.used = row
        self.unit = unit


SMALL = {"norm": 0, "second": 1, "misfit": 2, "energy": 3}


def make_emit(sh, pk, out_ref, prior):
    def emit(name, value):
        if name in SMALL:
            r = pk.at["small"][0] + SMALL[name]
            value = value if prior is None else value + prior[r : r + 1, :]
            out_ref[r : r + 1, :] = value
            return
        row, n = pk.at[name]
        if name == "embed":
            value = value[:n]
        pieces = [value]
        if name == "expand":
            pieces = [value[:, k : k + sh.width] for k in range(0, sh.hidden, sh.width)]
        for piece in pieces:
            m = piece.shape[0]
            add = piece if prior is None else piece + prior[row : row + m, :]
            out_ref[row : row + m, :] = add
            row += m

    return emit


def first_kernel(sh, *refs):
    ext, w, (new, *saved) = refs[0], refs[1:9], refs[9:]
    e = ext[...]
    closed, kept = forward(sh, e, w)
    new[...] = stencil(sh, e, closed)
    for ref, value in zip(saved, kept):
        ref[...] = value


def middle_kernel(sh, pk, *refs):
    ext, target, w, (back, packed) = refs[0], refs[1], refs[2:10], refs[10:12]
    packed[pk.at["small"][0] :, :] = jnp.zeros((pk.rows - pk.at["small"][0], sh.width), F32)
    emit = make_emit(sh, pk, packed, None)
    e = ext[...]
    closed, kept = forward(sh, e, w)
    goal = target[...]
    residue = stencil(sh, e, closed) - goal
    emit("misfit", jnp.sum(residue * residue, axis=0, keepdims=True))
    emit("energy", jnp.sum(goal * goal, axis=0, keepdims=True))
    backward(sh, e, w, kept, 2.0 * residue, back, emit)


def last_kernel(sh, pk, *refs):
    ext, cot, w, saved, prior, (back, packed) = refs[0], refs[1], refs[2:10], refs[10:19], refs[19], refs[20:22]
    packed[pk.at["small"][0] :, :] = prior[pk.at["small"][0] :, :]
    emit = make_emit(sh, pk, packed, prior)
    kept = tuple(ref[...] for ref in saved)
    backward(sh, ext[...], w, kept, cot[...], back, emit)


def neighbour(counts, dx, dy):
    nx, ny = counts
    return (
        lax.rem(lax.axis_index("gx") + (dx + nx), nx),
        lax.rem(lax.axis_index("gy") + (dy + ny), ny),
    )


def greet(devices):
    barrier = pltpu.get_barrier_semaphore()
    for device in devices:
        pl.semaphore_signal(barrier, inc=1, device_id=device, device_id_type=MESH)
    pl.semaphore_wait(barrier, len(devices))


AROUND = [(dx, dy) for dx in (-1, 0, 1) for dy in (-1, 0, 1) if (dx, dy) != (0, 0)]


def spread_kernel(sh, counts, u, ext, send, recv):
    greet([neighbour(counts, dx, dy) for dx, dy in AROUND])
    started = []
    for i, (dx, dy, src, dst, n) in enumerate(sh.copies()):
        copy = pltpu.make_async_remote_copy(
            src_ref=u.at[pl.ds(src, n)],
            dst_ref=ext.at[pl.ds(dst, n)],
            send_sem=send.at[i],
            recv_sem=recv.at[i],
            device_id=neighbour(counts, dx, dy),
            device_id_type=MESH,
        )
        copy.start()
        started.append(copy)
    at = 0
    for s, n in sh.view(0, 0):
        ext[s : s + n, :] = u[at : at + n, :]
        at += n
    for copy in started:
        copy.wait()


def gather_kernel(sh, counts, back, out, slots, send, recv):
    greet([neighbour(counts, dx, dy) for dx, dy in AROUND])
    end_gather(sh, back, out, slots, start_gather(sh, counts, back, slots, send, recv))


def exchange_orders(counts):
    nx, ny = counts
    bits = lambda n: [1 << k for k in range(n.bit_length() - 1)]
    ys = [("gy", s) for s in bits(ny)]
    xs = [("gx", s) for s in bits(nx)]
    head, y, x, z = ys[:1], ys[1:], xs[:1], xs[1:]
    return [head + y + x + z, head + x + z + y, head + z + y + x]


def partner(axis, s):
    gx, gy = lax.axis_index("gx"), lax.axis_index("gy")
    index = gx if axis == "gx" else gy
    bit = lax.rem(index // s, 2)
    other = index + s - 2 * s * bit
    return bit, ((other, gy) if axis == "gx" else (gx, other))


def start_gather(sh, counts, back, slots, send, recv):
    started = []
    place = 0
    for i, (dx, dy, dst, src, n) in enumerate(sh.copies()):
        copy = pltpu.make_async_remote_copy(
            src_ref=back.at[pl.ds(src, n)],
            dst_ref=slots.at[pl.ds(place, n)],
            send_sem=send.at[i],
            recv_sem=recv.at[i],
            device_id=neighbour(counts, -dx, -dy),
            device_id_type=MESH,
        )
        copy.start()
        started.append((copy, dst, place, n))
        place += n
    return started


def end_gather(sh, back, out, slots, started):
    at = 0
    for s, n in sh.view(0, 0):
        out[at : at + n, :] = back[s : s + n, :]
        at += n
    for copy, dst, place, n in started:
        copy.wait()
        out[dst : dst + n, :] += slots[place : place + n, :]


def reduce_kernel(sh, counts, parts, packed, back, out, cot, acc, slots, halo, send, recv, halo_send, halo_recv):
    orders = exchange_orders(counts)
    greet([neighbour(counts, dx, dy) for dx, dy in AROUND] + [partner(*step)[1] for step in orders[0]])
    halos = start_gather(sh, counts, back, halo, halo_send, halo_recv)
    steps = len(orders[0])
    where = []
    base = 0
    for order, start, rows in parts:
        where.append((start, rows, base))
        base += rows
    history = [[] for _ in parts]

    def halve(p, k):
        start, rows, base = where[p]
        bit, device = partner(*orders[parts[p][0]][k])
        half = rows // 2
        keep = pl.multiple_of(start + bit * half, 8)
        give = pl.multiple_of(start + half - bit * half, 8)
        source = packed if k == 0 else acc
        copy = pltpu.make_async_remote_copy(
            src_ref=source.at[pl.ds(give, half)],
            dst_ref=slots.at[pl.ds(base, half)],
            send_sem=send.at[p, k],
            recv_sem=recv.at[p, k],
            device_id=device,
            device_id_type=MESH,
        )
        copy.start()
        history[p].append((keep, half, device))
        return copy, source, keep, half, base

    def add(p, k, flight):
        copy, source, keep, half, base = flight
        copy.wait()
        target = acc if k < steps - 1 else out
        target[pl.ds(keep, half), :] = source[pl.ds(keep, half), :] + slots[pl.ds(base, half), :]
        where[p] = (keep, half, base + half)

    def collect(p, k):
        keep, half, device = history[p][k]
        copy = pltpu.make_async_remote_copy(
            src_ref=out.at[pl.ds(keep, half)],
            dst_ref=out.at[pl.ds(keep, half)],
            send_sem=send.at[p, steps + k],
            recv_sem=recv.at[p, steps + k],
            device_id=device,
            device_id_type=MESH,
        )
        copy.start()
        return copy

    every = range(len(parts))
    flights = [halve(p, 0) for p in every]
    end_gather(sh, back, cot, halo, halos)
    for k in range(steps):
        for p in every:
            add(p, k, flights[p])
            flights[p] = halve(p, k + 1) if k < steps - 1 else collect(p, k)
    for k in reversed(range(steps)):
        for p in every:
            flights[p].wait()
            if k > 0:
                flights[p] = collect(p, k - 1)


def finish_kernel(sh, pk, entries, packed, cot, loss, field, embed, norm, attend, output, second, expand, reduce, decode):
    small = pk.at["small"][0]
    energy = jnp.sum(packed[small + SMALL["energy"] : small + SMALL["energy"] + 1, :], axis=1, keepdims=True)
    misfit = jnp.sum(packed[small + SMALL["misfit"] : small + SMALL["misfit"] + 1, :], axis=1, keepdims=True)
    scale = entries / energy
    loss[...] = misfit / energy
    field[...] = scale * cot[...]
    norm[...] = scale * packed[small : small + 1, :]
    second[...] = scale * packed[small + 1 : small + 2, :]

    def piece(name):
        row, n = pk.at[name]
        return scale * packed[row : row + n, :]

    embed[...] = piece("embed")
    output[...] = piece("output")
    reduce[...] = piece("reduce")
    decode[...] = piece("decode")[:, : decode.shape[1]]
    d = sh.width
    for k, name in enumerate(("query", "key", "value")):
        attend[:, k * d : (k + 1) * d] = piece(name)
    row = pk.at["expand"][0]
    for k in range(sh.hidden // d):
        expand[:, k * d : (k + 1) * d] = scale * packed[row + k * d : row + (k + 1) * d, :]


def call(kernel, outs, args, scratch=(), collective=None):
    vm = pl.BlockSpec(memory_space=pltpu.VMEM)
    extra = {} if collective is None else dict(collective_id=collective, has_side_effects=True)
    return pl.pallas_call(
        kernel,
        out_shape=[jax.ShapeDtypeStruct(s, F32) for s in outs],
        in_specs=[vm] * len(args),
        out_specs=[vm] * len(outs),
        scratch_shapes=list(scratch),
        compiler_params=pltpu.CompilerParams(vmem_limit_bytes=VMEM_LIMIT, **extra),
    )(*args)


def to_tokens(sh, block):
    x = block.reshape(sh.ax, PATCH, sh.ay, PATCH, 3, sh.up, PATCH).transpose(0, 2, 5, 4, 1, 3, 6)
    return jnp.pad(x.reshape(sh.inner, 3 * sh.cube), ((0, 0), (0, sh.cube)))


def from_tokens(sh, tokens, shape):
    x = tokens[:, : 3 * sh.cube].reshape(sh.ax, sh.ay, sh.up, 3, PATCH, PATCH, PATCH)
    return x.transpose(0, 4, 1, 5, 3, 2, 6).reshape(shape)


def shards(counts, field, target, embed_weight, norm_gain, attend_weight, output_weight, second_gain, expand_weight, reduce_weight, decode_weight):
    width, hidden = expand_weight.shape
    sh = Shape(field.shape, width, hidden)
    devices = counts[0] * counts[1]
    pk = Packing(sh, devices)
    blocks = pk.rows // pk.unit
    cuts = [blocks * share // 10 for share in (0, 3, 5, 7, 8, 9, 10)]
    spans = zip((0, 1, 0, 2, 1, 2), cuts, cuts[1:])
    parts = [(order, a * pk.unit, (b - a) * pk.unit) for order, a, b in spans if b > a]
    weights = (
        jnp.pad(embed_weight, ((0, sh.cube), (0, 0))),
        norm_gain.reshape(1, width),
        attend_weight,
        output_weight,
        second_gain.reshape(1, width),
        expand_weight,
        reduce_weight,
        jnp.pad(decode_weight, ((0, 0), (0, sh.cube))),
    )
    ext_shape, inner_shape = (sh.ext, sh.feat), (sh.inner, sh.feat)
    slabs = sh.copies()
    sems = [pltpu.SemaphoreType.DMA((len(slabs),))] * 2
    slot_rows = sum(s[4] for s in slabs)

    def spread(u):
        return call(functools.partial(spread_kernel, sh, counts), [ext_shape], (u,), sems, 1)[0]

    def gather(back):
        scratch = [pltpu.VMEM((slot_rows, sh.feat), F32)] + sems
        return call(functools.partial(gather_kernel, sh, counts), [inner_shape], (back,), scratch, 2)[0]

    tokens_shape, query_shape = (sh.ext, width), (sh.inner, width)
    saved_shapes = [
        tokens_shape,
        query_shape,
        tokens_shape,
        tokens_shape,
        (HEADS * sh.inner, sh.ext),
        query_shape,
        query_shape,
        (sh.inner, hidden),
        query_shape,
    ]
    goal = to_tokens(sh, target)
    ext0 = spread(to_tokens(sh, field))
    new, *saved = call(functools.partial(first_kernel, sh), [inner_shape] + saved_shapes, (ext0,) + weights)
    ext1 = spread(new)
    packed_shape = (pk.rows, width)
    back, packed = call(functools.partial(middle_kernel, sh, pk), [ext_shape, packed_shape], (ext1, goal) + weights)
    cot = gather(back)
    back, packed = call(
        functools.partial(last_kernel, sh, pk),
        [ext_shape, packed_shape],
        (ext0, cot) + weights + tuple(saved) + (packed,),
    )
    steps = len(exchange_orders(counts)[0])
    summed, cot = call(
        functools.partial(reduce_kernel, sh, counts, parts),
        [packed_shape, inner_shape],
        (packed, back),
        [
            pltpu.VMEM(packed_shape, F32),
            pltpu.VMEM(packed_shape, F32),
            pltpu.VMEM((slot_rows, sh.feat), F32),
        ]
        + [pltpu.SemaphoreType.DMA((len(parts), 2 * steps))] * 2
        + sems,
        3,
    )
    entries = float(np.prod(field.shape) * devices)
    params = (embed_weight, norm_gain, attend_weight, output_weight, second_gain, expand_weight, reduce_weight, decode_weight)
    outs = [(1, 1), inner_shape] + [p.shape if p.ndim == 2 else (1, width) for p in params]
    done = call(functools.partial(finish_kernel, sh, pk, entries), outs, (summed, cot))
    grads = tuple(g.reshape(p.shape) for g, p in zip(done[2:], params))
    return (done[0].reshape(()), from_tokens(sh, done[1], field.shape)) + grads


def solution(mesh):
    counts = (mesh.shape["gx"], mesh.shape["gy"])
    in_specs = (P("gx", "gy", None), P("gx", "gy", None), P(), P(), P(), P(), P(), P(), P(), P())
    out_specs = (P(), P("gx", "gy", None), P(), P(), P(), P(), P(), P(), P(), P())
    return jax.shard_map(
        functools.partial(shards, counts), mesh=mesh, in_specs=in_specs, out_specs=out_specs, check_vma=False
    )
```

```python
import functools

import jax
import jax.numpy as jnp
import numpy as np
from jax import lax
from jax.experimental import pallas as pl
from jax.experimental.pallas import tpu as pltpu
from jax.sharding import PartitionSpec as P

PATCH = 4
HEADS = 8
STEPS = 2

EPSILON = 1e-06
TIME_STEP = 0.1
VISCOSITY = 0.5
LANES = 128
MESH = pl.DeviceIdType.MESH
VMEM_LIMIT = 56 * 1024 * 1024
F32 = jnp.float32


def dot(left, right, dims):
    lh = left.astype(jnp.bfloat16)
    rh = right.astype(jnp.bfloat16)
    ll = (left - lh.astype(F32)).astype(jnp.bfloat16)
    rl = (right - rh.astype(F32)).astype(jnp.bfloat16)
    one = lambda a, b: lax.dot_general(a, b, (dims, ((), ())), preferred_element_type=F32)
    return one(lh, rh) + (one(lh, rl) + one(ll, rh))


def nn(a, b):
    return dot(a, b, ((1,), (0,)))


def nt(a, b):
    return dot(a, b, ((1,), (1,)))


def tn(a, b):
    return dot(a, b, ((0,), (0,)))


class Shape:
    def __init__(self, field_shape, width, hidden):
        wide, tall, depth = field_shape
        self.ax, self.ay, self.up = wide // PATCH, tall // PATCH, depth // 3 // PATCH
        self.ex, self.ey = self.ax + 2, self.ay + 2
        self.inner = self.ax * self.ay * self.up
        self.ext = self.ex * self.ey * self.up
        self.cube = PATCH**3
        self.feat = 4 * self.cube
        self.width, self.hidden = width, hidden

    def row(self, x, y):
        return (x * self.ey + y) * self.up

    def view(self, dx, dy):
        return [(self.row(x + 1 + dx, 1 + dy), self.ay * self.up) for x in range(self.ax)]

    def copies(self):
        out = []
        for dx in (-1, 0, 1):
            for dy in (-1, 0, 1):
                if dx == 0 and dy == 0:
                    continue
                xs = {1: [(self.ax - 1, 0)], -1: [(0, self.ex - 1)], 0: [(x, x + 1) for x in range(self.ax)]}[dx]
                ys = {1: (self.ay - 1, 0, 1), -1: (0, self.ey - 1, 1), 0: (0, 1, self.ay)}[dy]
                for src, dst in xs:
                    out.append(
                        (dx, dy, (src * self.ay + ys[0]) * self.up, self.row(dst, ys[1]), ys[2] * self.up)
                    )
        return out


def take(value, spans):
    return jnp.concatenate([value[s : s + n] for s, n in spans], axis=0)


def lroll(value, shift):
    return pltpu.roll(value, shift % value.shape[1], 1)


def iota(shape, dim):
    return lax.broadcasted_iota(jnp.int32, shape, dim)


def stencil_parts(sh, ext):
    shape = (sh.inner, sh.feat)
    lane = iota(shape, 1)
    px, py, pz = (lane // (PATCH * PATCH)) % PATCH, (lane // PATCH) % PATCH, lane % PATCH
    comp = lane // sh.cube
    level = iota(shape, 0) % sh.up
    u = take(ext, sh.view(0, 0))
    last = PATCH - 1

    def plus(here, there, pos, stride):
        return jnp.where(pos < last, lroll(here, -stride), lroll(there, last * stride))

    def minus(here, there, pos, stride):
        return jnp.where(pos > 0, lroll(here, stride), lroll(there, -last * stride))

    above = jnp.where(level == sh.up - 1, 0.0, pltpu.roll(u, sh.inner - 1, 0))
    below = jnp.where(level == 0, 0.0, pltpu.roll(u, 1, 0))
    sx, sy = PATCH * PATCH, PATCH
    east = plus(u, take(ext, sh.view(1, 0)), px, sx)
    west = minus(u, take(ext, sh.view(-1, 0)), px, sx)
    north = plus(u, take(ext, sh.view(0, 1)), py, sy)
    south = minus(u, take(ext, sh.view(0, -1)), py, sy)
    upper = plus(u, above, pz, 1)
    lower = minus(u, below, pz, 1)
    r1, r2, r3 = lroll(u, sh.cube), lroll(u, 2 * sh.cube), lroll(u, 3 * sh.cube)
    first, second = comp == 0, comp == 1
    vx = jnp.where(first, u, jnp.where(second, r1, r2))
    vy = jnp.where(first, r3, jnp.where(second, u, r1))
    vz = jnp.where(first, r2, jnp.where(second, r3, u))
    return u, (east, west, north, south, upper, lower), (vx, vy, vz), (px, py, pz, comp, level)


def stencil(sh, ext, closed):
    u, (east, west, north, south, upper, lower), (vx, vy, vz), _ = stencil_parts(sh, ext)
    laplace = east + west + north + south + upper + lower - 6.0 * u
    carried = 0.5 * (vx * (east - west) + vy * (north - south) + vz * (upper - lower))
    return u + TIME_STEP * (VISCOSITY * laplace - carried + closed)


def stencil_back(sh, ext, cot, out_ref):
    u, (east, west, north, south, upper, lower), (vx, vy, vz), where = stencil_parts(sh, ext)
    px, py, pz, comp, level = where
    g = TIME_STEP * cot
    total = cot - (6.0 * VISCOSITY) * g

    def summed(value):
        return (
            value
            + lroll(value, sh.cube)
            + lroll(value, 2 * sh.cube)
            + lroll(value, 3 * sh.cube)
        )

    fx = summed(-0.5 * g * (east - west))
    fy = summed(-0.5 * g * (north - south))
    fz = summed(-0.5 * g * (upper - lower))
    total += jnp.where(comp == 0, fx, jnp.where(comp == 1, fy, jnp.where(comp == 2, fz, 0.0)))
    last = PATCH - 1

    def sides(pos, stride, speed):
        high = g * (VISCOSITY - 0.5 * speed)
        low = g * (VISCOSITY + 0.5 * speed)
        here = lroll(jnp.where(pos < last, high, 0.0), stride) + lroll(jnp.where(pos > 0, low, 0.0), -stride)
        after = lroll(jnp.where(pos == last, high, 0.0), -last * stride)
        before = lroll(jnp.where(pos == 0, low, 0.0), last * stride)
        return here, after, before

    here, east_back, west_back = sides(px, PATCH * PATCH, vx)
    total += here
    here, north_back, south_back = sides(py, PATCH, vy)
    total += here
    here, above_back, below_back = sides(pz, 1, vz)
    total += here
    total += jnp.where(level == 0, 0.0, pltpu.roll(above_back, 1, 0))
    total += jnp.where(level == sh.up - 1, 0.0, pltpu.roll(below_back, sh.inner - 1, 0))
    for value, shift in (
        (total, (0, 0)),
        (east_back, (1, 0)),
        (west_back, (-1, 0)),
        (north_back, (0, 1)),
        (south_back, (0, -1)),
    ):
        at = 0
        for s, n in sh.view(*shift):
            out_ref[s : s + n, :] += value[at : at + n]
            at += n


def head_split(sh, value):
    head = iota(value.shape, 1) // (sh.width // HEADS)
    return jnp.concatenate([jnp.where(head == h, value, 0.0) for h in range(HEADS)], axis=0)


def head_join(sh, value):
    head = iota((sh.inner, sh.width), 1) // (sh.width // HEADS)
    total = jnp.zeros((sh.inner, sh.width), F32)
    for h in range(HEADS):
        total = jnp.where(head == h, value[h * sh.inner : (h + 1) * sh.inner], total)
    return total


def inverse_rms(value):
    return lax.rsqrt(jnp.mean(value * value, axis=-1, keepdims=True) + EPSILON)


def forward(sh, ext, w):
    we, g1, wa, wo, g2, wx, wr, wd = w
    d = sh.width
    tokens = nn(ext, we[...])
    normed = tokens * inverse_rms(tokens) * g1[...]
    queries = nn(take(normed, sh.view(0, 0)), wa[:, :d])
    mixed = nn(normed, wa[:, d:])
    keys, values = mixed[:, :d], mixed[:, d:]
    shape = (HEADS * sh.inner, sh.ext)
    qcol = (iota(shape, 0) % sh.inner) // sh.up
    kcol = iota(shape, 1) // sh.up
    dx = kcol // sh.ey - qcol // sh.ay
    dy = kcol % sh.ey - qcol % sh.ay
    seen = (dx >= 0) & (dx <= 2) & (dy >= 0) & (dy <= 2)
    scores = nt(head_split(sh, queries), keys) * ((d // HEADS) ** -0.5)
    weights = jnp.exp(jnp.where(seen, scores, -1e30))
    weights = weights / jnp.sum(weights, axis=-1, keepdims=True)
    attended = head_join(sh, nn(weights, values))
    mid = take(tokens, sh.view(0, 0)) + nn(attended, wo[...])
    pre = nn(mid * inverse_rms(mid) * g2[...], wx[...])
    late = mid + nn(pre / (1.0 + jnp.exp(-pre)), wr[...])
    return nn(late, wd[...]), (tokens, queries, keys, values, weights, attended, mid, pre, late)


def backward(sh, ext, w, saved, cot, back_ref, emit):
    we, g1, wa, wo, g2, wx, wr, wd = w
    d = sh.width
    tokens, queries, keys, values, weights, attended, mid, pre, late = saved
    dclosed = TIME_STEP * cot
    emit("decode", tn(late, dclosed))
    dlate = nt(dclosed, wd[...])
    sig = 1.0 / (1.0 + jnp.exp(-pre))
    emit("reduce", tn(pre * sig, dlate))
    dpre = nt(dlate, wr[...]) * (sig * (1.0 + pre * (1.0 - sig)))
    r2 = inverse_rms(mid)
    unit = mid * r2
    emit("expand", tn(unit * g2[...], dpre))
    dn = nt(dpre, wx[...])
    emit("second", jnp.sum(dn * unit, axis=0, keepdims=True))
    y = dn * g2[...]
    dmid = dlate + r2 * (y - unit * jnp.mean(y * unit, axis=-1, keepdims=True))
    emit("output", tn(attended, dmid))
    dsplit = head_split(sh, nt(dmid, wo[...]))
    dweights = nt(dsplit, values)
    dvalues = tn(weights, dsplit)
    dscores = weights * (dweights - jnp.sum(dweights * weights, axis=-1, keepdims=True))
    dscores = dscores * ((d // HEADS) ** -0.5)
    dqueries = head_join(sh, nn(dscores, keys))
    dkeys = tn(dscores, head_split(sh, queries))
    r1 = inverse_rms(tokens)
    unit = tokens * r1
    normed = unit * g1[...]
    emit("query", tn(take(normed, sh.view(0, 0)), dqueries))
    emit("key", tn(normed, dkeys))
    emit("value", tn(normed, dvalues))
    dn = nt(dkeys, wa[:, d : 2 * d]) + nt(dvalues, wa[:, 2 * d :])
    dinner = nt(dqueries, wa[:, :d])
    back_ref[...] = dn
    at = 0
    for s, n in sh.view(0, 0):
        back_ref[s : s + n, :] += dinner[at : at + n]
        at += n
    dn = back_ref[...]
    emit("norm", jnp.sum(dn * unit, axis=0, keepdims=True))
    y = dn * g1[...]
    back_ref[...] = r1 * (y - unit * jnp.mean(y * unit, axis=-1, keepdims=True))
    at = 0
    for s, n in sh.view(0, 0):
        back_ref[s : s + n, :] += dmid[at : at + n]
        at += n
    dtokens = back_ref[...]
    emit("embed", tn(ext, dtokens))
    back_ref[...] = nt(dtokens, we[...])
    stencil_back(sh, ext, cot, back_ref)


class Packing:
    def __init__(self, sh, devices):
        d = sh.width
        sizes = [
            ("reduce", sh.hidden),
            ("expand", d * (sh.hidden // d)),
            ("decode", d),
            ("output", d),
            ("query", d),
            ("key", d),
            ("value", d),
            ("embed", sh.feat - sh.cube),
            ("small", 8),
        ]
        self.at, row = {}, 0
        for name, n in sizes:
            self.at[name] = (row, n)
            row += n
        unit = 8 * devices
        self.rows = -(-row // unit) * unit
        self.used = row
        self.unit = unit


SMALL = {"norm": 0, "second": 1, "misfit": 2, "energy": 3}


def make_emit(sh, pk, out_ref, prior):
    def emit(name, value):
        if name in SMALL:
            r = pk.at["small"][0] + SMALL[name]
            value = value if prior is None else value + prior[r : r + 1, :]
            out_ref[r : r + 1, :] = value
            return
        row, n = pk.at[name]
        if name == "embed":
            value = value[:n]
        pieces = [value]
        if name == "expand":
            pieces = [value[:, k : k + sh.width] for k in range(0, sh.hidden, sh.width)]
        for piece in pieces:
            m = piece.shape[0]
            add = piece if prior is None else piece + prior[row : row + m, :]
            out_ref[row : row + m, :] = add
            row += m

    return emit


def neighbour(counts, dx, dy):
    nx, ny = counts
    return (
        lax.rem(lax.axis_index("gx") + (dx + nx), nx),
        lax.rem(lax.axis_index("gy") + (dy + ny), ny),
    )


def greet(devices):
    barrier = pltpu.get_barrier_semaphore()
    for device in devices:
        pl.semaphore_signal(barrier, inc=1, device_id=device, device_id_type=MESH)
    pl.semaphore_wait(barrier, len(devices))


AROUND = [(dx, dy) for dx in (-1, 0, 1) for dy in (-1, 0, 1) if (dx, dy) != (0, 0)]


def spread(sh, counts, u, ext, send, recv):
    started = []
    for i, (dx, dy, src, dst, n) in enumerate(sh.copies()):
        copy = pltpu.make_async_remote_copy(
            src_ref=u.at[pl.ds(src, n)],
            dst_ref=ext.at[pl.ds(dst, n)],
            send_sem=send.at[i],
            recv_sem=recv.at[i],
            device_id=neighbour(counts, dx, dy),
            device_id_type=MESH,
        )
        copy.start()
        started.append(copy)
    at = 0
    for s, n in sh.view(0, 0):
        ext[s : s + n, :] = u[at : at + n, :]
        at += n
    for copy in started:
        copy.wait()


def exchange_orders(counts):
    nx, ny = counts
    bits = lambda n: [1 << k for k in range(n.bit_length() - 1)]
    ys = [("gy", s) for s in bits(ny)]
    xs = [("gx", s) for s in bits(nx)]
    head, y, x, z = ys[:1], ys[1:], xs[:1], xs[1:]
    return [head + y + x + z, head + x + z + y, head + z + y + x]


def partner(axis, s):
    gx, gy = lax.axis_index("gx"), lax.axis_index("gy")
    index = gx if axis == "gx" else gy
    bit = lax.rem(index // s, 2)
    other = index + s - 2 * s * bit
    return bit, ((other, gy) if axis == "gx" else (gx, other))


def start_gather(sh, counts, back, slots, send, recv):
    started = []
    place = 0
    for i, (dx, dy, dst, src, n) in enumerate(sh.copies()):
        copy = pltpu.make_async_remote_copy(
            src_ref=back.at[pl.ds(src, n)],
            dst_ref=slots.at[pl.ds(place, n)],
            send_sem=send.at[i],
            recv_sem=recv.at[i],
            device_id=neighbour(counts, -dx, -dy),
            device_id_type=MESH,
        )
        copy.start()
        started.append((copy, dst, place, n))
        place += n
    return started


def end_gather(sh, back, out, slots, started):
    at = 0
    for s, n in sh.view(0, 0):
        out[at : at + n, :] = back[s : s + n, :]
        at += n
    for copy, dst, place, n in started:
        copy.wait()
        out[dst : dst + n, :] += slots[place : place + n, :]


def steps_kernel(sh, pk, counts, parts, *refs):
    u0, goal, w, (out, cot0) = refs[0], refs[1], refs[2:10], refs[10:12]
    ext0, ext1, u1, back1, back0, cot1, packed, acc, slots, halo1, halo0 = refs[12:23]
    saved, (send, recv, spread_send, spread_recv, gather_send, gather_recv) = refs[23:32], refs[32:38]
    orders = exchange_orders(counts)
    greet([neighbour(counts, dx, dy) for dx, dy in AROUND] + [partner(*step)[1] for step in orders[0]])
    spread(sh, counts, u0, ext0, spread_send.at[0], spread_recv.at[0])
    closed, kept = forward(sh, ext0[...], w)
    u1[...] = stencil(sh, ext0[...], closed)
    for ref, value in zip(saved, kept):
        ref[...] = value
    spread(sh, counts, u1, ext1, spread_send.at[1], spread_recv.at[1])
    packed[pk.at["small"][0] :, :] = jnp.zeros((pk.rows - pk.at["small"][0], sh.width), F32)
    emit = make_emit(sh, pk, packed, None)
    closed, kept = forward(sh, ext1[...], w)
    residue = stencil(sh, ext1[...], closed) - goal[...]
    emit("misfit", jnp.sum(residue * residue, axis=0, keepdims=True))
    emit("energy", jnp.sum(goal[...] * goal[...], axis=0, keepdims=True))
    backward(sh, ext1[...], w, kept, 2.0 * residue, back1, emit)
    end_gather(sh, back1, cot1, halo1, start_gather(sh, counts, back1, halo1, gather_send.at[0], gather_recv.at[0]))
    steps = len(orders[0])
    where = []
    base = 0
    for order, start, rows in parts:
        where.append((start, rows, base))
        base += rows
    history = [[] for _ in parts]

    def halve(p, k):
        start, rows, base = where[p]
        bit, device = partner(*orders[parts[p][0]][k])
        half = rows // 2
        keep = pl.multiple_of(start + bit * half, 8)
        give = pl.multiple_of(start + half - bit * half, 8)
        source = packed if k == 0 else acc
        copy = pltpu.make_async_remote_copy(
            src_ref=source.at[pl.ds(give, half)],
            dst_ref=slots.at[pl.ds(base, half)],
            send_sem=send.at[p, k],
            recv_sem=recv.at[p, k],
            device_id=device,
            device_id_type=MESH,
        )
        copy.start()
        history[p].append((keep, half, device))
        return copy, source, keep, half, base

    def add(p, k, flight):
        copy, source, keep, half, base = flight
        copy.wait()
        target = acc if k < steps - 1 else out
        target[pl.ds(keep, half), :] = source[pl.ds(keep, half), :] + slots[pl.ds(base, half), :]
        where[p] = (keep, half, base + half)

    def collect(p, k):
        keep, half, device = history[p][k]
        copy = pltpu.make_async_remote_copy(
            src_ref=out.at[pl.ds(keep, half)],
            dst_ref=out.at[pl.ds(keep, half)],
            send_sem=send.at[p, steps + k],
            recv_sem=recv.at[p, steps + k],
            device_id=device,
            device_id_type=MESH,
        )
        copy.start()
        return copy

    every = range(len(parts))
    first = pk.at["query"][0]
    early = [p for p in every if parts[p][1] + parts[p][2] <= first]
    flights = {}
    emit = make_emit(sh, pk, packed, packed)

    def emit_and_send(name, value):
        emit(name, value)
        if name == "output":
            for p in early:
                flights[p] = halve(p, 0)
        if name == "query":
            for p in early:
                add(p, 0, flights[p])
                flights[p] = halve(p, 1)

    backward(sh, ext0[...], w, tuple(ref[...] for ref in saved), cot1[...], back0, emit_and_send)
    halos = start_gather(sh, counts, back0, halo0, gather_send.at[1], gather_recv.at[1])
    for p in every:
        if p not in early:
            flights[p] = halve(p, 0)
    end_gather(sh, back0, cot0, halo0, halos)
    for k in range(steps):
        for p in every:
            if k == 0 and p in early:
                continue
            add(p, k, flights[p])
            flights[p] = halve(p, k + 1) if k < steps - 1 else collect(p, k)
    for k in reversed(range(steps)):
        for p in every:
            flights[p].wait()
            if k > 0:
                flights[p] = collect(p, k - 1)


def finish_kernel(sh, pk, entries, packed, cot, loss, field, embed, norm, attend, output, second, expand, reduce, decode):
    small = pk.at["small"][0]
    energy = jnp.sum(packed[small + SMALL["energy"] : small + SMALL["energy"] + 1, :], axis=1, keepdims=True)
    misfit = jnp.sum(packed[small + SMALL["misfit"] : small + SMALL["misfit"] + 1, :], axis=1, keepdims=True)
    scale = entries / energy
    loss[...] = misfit / energy
    field[...] = scale * cot[...]
    norm[...] = scale * packed[small : small + 1, :]
    second[...] = scale * packed[small + 1 : small + 2, :]

    def piece(name):
        row, n = pk.at[name]
        return scale * packed[row : row + n, :]

    embed[...] = piece("embed")
    output[...] = piece("output")
    reduce[...] = piece("reduce")
    decode[...] = piece("decode")[:, : decode.shape[1]]
    d = sh.width
    for k, name in enumerate(("query", "key", "value")):
        attend[:, k * d : (k + 1) * d] = piece(name)
    row = pk.at["expand"][0]
    for k in range(sh.hidden // d):
        expand[:, k * d : (k + 1) * d] = scale * packed[row + k * d : row + (k + 1) * d, :]


def call(kernel, outs, args, scratch=(), collective=None):
    vm = pl.BlockSpec(memory_space=pltpu.VMEM)
    extra = {} if collective is None else dict(collective_id=collective, has_side_effects=True)
    return pl.pallas_call(
        kernel,
        out_shape=[jax.ShapeDtypeStruct(s, F32) for s in outs],
        in_specs=[vm] * len(args),
        out_specs=[vm] * len(outs),
        scratch_shapes=list(scratch),
        compiler_params=pltpu.CompilerParams(vmem_limit_bytes=VMEM_LIMIT, **extra),
    )(*args)


def to_tokens(sh, block):
    x = block.reshape(sh.ax, PATCH, sh.ay, PATCH, 3, sh.up, PATCH).transpose(0, 2, 5, 4, 1, 3, 6)
    return jnp.pad(x.reshape(sh.inner, 3 * sh.cube), ((0, 0), (0, sh.cube)))


def from_tokens(sh, tokens, shape):
    x = tokens[:, : 3 * sh.cube].reshape(sh.ax, sh.ay, sh.up, 3, PATCH, PATCH, PATCH)
    return x.transpose(0, 4, 1, 5, 3, 2, 6).reshape(shape)


def shards(counts, field, target, embed_weight, norm_gain, attend_weight, output_weight, second_gain, expand_weight, reduce_weight, decode_weight):
    width, hidden = expand_weight.shape
    sh = Shape(field.shape, width, hidden)
    devices = counts[0] * counts[1]
    pk = Packing(sh, devices)
    blocks = pk.rows // pk.unit
    cuts = [blocks * share // 10 for share in (0, 3, 5, 6, 8, 9, 10)]
    spans = zip((0, 1, 2, 0, 1, 2), cuts, cuts[1:])
    parts = [(order, a * pk.unit, (b - a) * pk.unit) for order, a, b in spans if b > a]
    weights = (
        jnp.pad(embed_weight, ((0, sh.cube), (0, 0))),
        norm_gain.reshape(1, width),
        attend_weight,
        output_weight,
        second_gain.reshape(1, width),
        expand_weight,
        reduce_weight,
        jnp.pad(decode_weight, ((0, 0), (0, sh.cube))),
    )
    ext_shape, inner_shape = (sh.ext, sh.feat), (sh.inner, sh.feat)
    slabs = sh.copies()
    sems = [pltpu.SemaphoreType.DMA((2, len(slabs)))] * 4
    slot_rows = sum(n[4] for n in slabs)
    tokens_shape, query_shape = (sh.ext, width), (sh.inner, width)
    saved_shapes = [
        tokens_shape,
        query_shape,
        tokens_shape,
        tokens_shape,
        (HEADS * sh.inner, sh.ext),
        query_shape,
        query_shape,
        (sh.inner, hidden),
        query_shape,
    ]
    goal = to_tokens(sh, target)
    packed_shape = (pk.rows, width)
    steps = len(exchange_orders(counts)[0])
    halo_shape = (slot_rows, sh.feat)
    scratch = [ext_shape, ext_shape, inner_shape, ext_shape, ext_shape, inner_shape] + [packed_shape] * 3
    scratch += [halo_shape] * 2 + saved_shapes
    summed, cot = call(
        functools.partial(steps_kernel, sh, pk, counts, parts),
        [packed_shape, inner_shape],
        (to_tokens(sh, field), goal) + weights,
        [pltpu.VMEM(shape, F32) for shape in scratch]
        + [pltpu.SemaphoreType.DMA((len(parts), 2 * steps))] * 2
        + sems,
        1,
    )
    entries = float(np.prod(field.shape) * devices)
    params = (embed_weight, norm_gain, attend_weight, output_weight, second_gain, expand_weight, reduce_weight, decode_weight)
    outs = [(1, 1), inner_shape] + [p.shape if p.ndim == 2 else (1, width) for p in params]
    done = call(functools.partial(finish_kernel, sh, pk, entries), outs, (summed, cot))
    grads = tuple(g.reshape(p.shape) for g, p in zip(done[2:], params))
    return (done[0].reshape(()), from_tokens(sh, done[1], field.shape)) + grads


def solution(mesh):
    counts = (mesh.shape["gx"], mesh.shape["gy"])
    in_specs = (P("gx", "gy", None), P("gx", "gy", None), P(), P(), P(), P(), P(), P(), P(), P())
    out_specs = (P(), P("gx", "gy", None), P(), P(), P(), P(), P(), P(), P(), P())
    return jax.shard_map(
        functools.partial(shards, counts), mesh=mesh, in_specs=in_specs, out_specs=out_specs, check_vma=False
    )
```

```python
import functools

import jax
import jax.numpy as jnp
import numpy as np
from jax import lax
from jax.experimental import pallas as pl
from jax.experimental.pallas import tpu as pltpu
from jax.sharding import PartitionSpec as P

PATCH = 4
HEADS = 8
STEPS = 2

EPSILON = 1e-06
TIME_STEP = 0.1
VISCOSITY = 0.5
LANES = 128
MESH = pl.DeviceIdType.MESH
VMEM_LIMIT = 56 * 1024 * 1024
F32 = jnp.float32


def dot(left, right, dims):
    lh = left.astype(jnp.bfloat16)
    rh = right.astype(jnp.bfloat16)
    ll = (left - lh.astype(F32)).astype(jnp.bfloat16)
    rl = (right - rh.astype(F32)).astype(jnp.bfloat16)
    one = lambda a, b: lax.dot_general(a, b, (dims, ((), ())), preferred_element_type=F32)
    return one(lh, rh) + (one(lh, rl) + one(ll, rh))


def nn(a, b):
    return dot(a, b, ((1,), (0,)))


def nt(a, b):
    return dot(a, b, ((1,), (1,)))


def tn(a, b):
    return dot(a, b, ((0,), (0,)))


class Shape:
    def __init__(self, field_shape, width, hidden):
        wide, tall, depth = field_shape
        self.ax, self.ay, self.up = wide // PATCH, tall // PATCH, depth // 3 // PATCH
        self.ex, self.ey = self.ax + 2, self.ay + 2
        self.inner = self.ax * self.ay * self.up
        self.ext = self.ex * self.ey * self.up
        self.cube = PATCH**3
        self.feat = 4 * self.cube
        self.width, self.hidden = width, hidden

    def row(self, x, y):
        return (x * self.ey + y) * self.up

    def view(self, dx, dy):
        return [(self.row(x + 1 + dx, 1 + dy), self.ay * self.up) for x in range(self.ax)]

    def copies(self):
        out = []
        for dx in (-1, 0, 1):
            for dy in (-1, 0, 1):
                if dx == 0 and dy == 0:
                    continue
                xs = {1: [(self.ax - 1, 0)], -1: [(0, self.ex - 1)], 0: [(x, x + 1) for x in range(self.ax)]}[dx]
                ys = {1: (self.ay - 1, 0, 1), -1: (0, self.ey - 1, 1), 0: (0, 1, self.ay)}[dy]
                for src, dst in xs:
                    out.append(
                        (dx, dy, (src * self.ay + ys[0]) * self.up, self.row(dst, ys[1]), ys[2] * self.up)
                    )
        return out


def take(value, spans):
    return jnp.concatenate([value[s : s + n] for s, n in spans], axis=0)


def lroll(value, shift):
    return pltpu.roll(value, shift % value.shape[1], 1)


def iota(shape, dim):
    return lax.broadcasted_iota(jnp.int32, shape, dim)


def stencil_parts(sh, ext):
    shape = (sh.inner, sh.feat)
    lane = iota(shape, 1)
    px, py, pz = (lane // (PATCH * PATCH)) % PATCH, (lane // PATCH) % PATCH, lane % PATCH
    comp = lane // sh.cube
    level = iota(shape, 0) % sh.up
    u = take(ext, sh.view(0, 0))
    last = PATCH - 1

    def plus(here, there, pos, stride):
        return jnp.where(pos < last, lroll(here, -stride), lroll(there, last * stride))

    def minus(here, there, pos, stride):
        return jnp.where(pos > 0, lroll(here, stride), lroll(there, -last * stride))

    above = jnp.where(level == sh.up - 1, 0.0, pltpu.roll(u, sh.inner - 1, 0))
    below = jnp.where(level == 0, 0.0, pltpu.roll(u, 1, 0))
    sx, sy = PATCH * PATCH, PATCH
    east = plus(u, take(ext, sh.view(1, 0)), px, sx)
    west = minus(u, take(ext, sh.view(-1, 0)), px, sx)
    north = plus(u, take(ext, sh.view(0, 1)), py, sy)
    south = minus(u, take(ext, sh.view(0, -1)), py, sy)
    upper = plus(u, above, pz, 1)
    lower = minus(u, below, pz, 1)
    r1, r2, r3 = lroll(u, sh.cube), lroll(u, 2 * sh.cube), lroll(u, 3 * sh.cube)
    first, second = comp == 0, comp == 1
    vx = jnp.where(first, u, jnp.where(second, r1, r2))
    vy = jnp.where(first, r3, jnp.where(second, u, r1))
    vz = jnp.where(first, r2, jnp.where(second, r3, u))
    return u, (east, west, north, south, upper, lower), (vx, vy, vz), (px, py, pz, comp, level)


def stencil(sh, ext, closed):
    u, (east, west, north, south, upper, lower), (vx, vy, vz), _ = stencil_parts(sh, ext)
    laplace = east + west + north + south + upper + lower - 6.0 * u
    carried = 0.5 * (vx * (east - west) + vy * (north - south) + vz * (upper - lower))
    return u + TIME_STEP * (VISCOSITY * laplace - carried + closed)


def stencil_back(sh, ext, cot, out_ref):
    u, (east, west, north, south, upper, lower), (vx, vy, vz), where = stencil_parts(sh, ext)
    px, py, pz, comp, level = where
    g = TIME_STEP * cot
    total = cot - (6.0 * VISCOSITY) * g

    def summed(value):
        return (
            value
            + lroll(value, sh.cube)
            + lroll(value, 2 * sh.cube)
            + lroll(value, 3 * sh.cube)
        )

    fx = summed(-0.5 * g * (east - west))
    fy = summed(-0.5 * g * (north - south))
    fz = summed(-0.5 * g * (upper - lower))
    total += jnp.where(comp == 0, fx, jnp.where(comp == 1, fy, jnp.where(comp == 2, fz, 0.0)))
    last = PATCH - 1

    def sides(pos, stride, speed):
        high = g * (VISCOSITY - 0.5 * speed)
        low = g * (VISCOSITY + 0.5 * speed)
        here = lroll(jnp.where(pos < last, high, 0.0), stride) + lroll(jnp.where(pos > 0, low, 0.0), -stride)
        after = lroll(jnp.where(pos == last, high, 0.0), -last * stride)
        before = lroll(jnp.where(pos == 0, low, 0.0), last * stride)
        return here, after, before

    here, east_back, west_back = sides(px, PATCH * PATCH, vx)
    total += here
    here, north_back, south_back = sides(py, PATCH, vy)
    total += here
    here, above_back, below_back = sides(pz, 1, vz)
    total += here
    total += jnp.where(level == 0, 0.0, pltpu.roll(above_back, 1, 0))
    total += jnp.where(level == sh.up - 1, 0.0, pltpu.roll(below_back, sh.inner - 1, 0))
    for value, shift in (
        (total, (0, 0)),
        (east_back, (1, 0)),
        (west_back, (-1, 0)),
        (north_back, (0, 1)),
        (south_back, (0, -1)),
    ):
        at = 0
        for s, n in sh.view(*shift):
            out_ref[s : s + n, :] += value[at : at + n]
            at += n


def head_split(sh, value):
    head = iota(value.shape, 1) // (sh.width // HEADS)
    return jnp.concatenate([jnp.where(head == h, value, 0.0) for h in range(HEADS)], axis=0)


def head_join(sh, value):
    head = iota((sh.inner, sh.width), 1) // (sh.width // HEADS)
    total = jnp.zeros((sh.inner, sh.width), F32)
    for h in range(HEADS):
        total = jnp.where(head == h, value[h * sh.inner : (h + 1) * sh.inner], total)
    return total


def inverse_rms(value):
    return lax.rsqrt(jnp.mean(value * value, axis=-1, keepdims=True) + EPSILON)


def forward(sh, ext, w):
    we, g1, wa, wo, g2, wx, wr, wd = w
    d = sh.width
    tokens = nn(ext, we[...])
    normed = tokens * inverse_rms(tokens) * g1[...]
    queries = nn(take(normed, sh.view(0, 0)), wa[:, :d])
    mixed = nn(normed, wa[:, d:])
    keys, values = mixed[:, :d], mixed[:, d:]
    shape = (HEADS * sh.inner, sh.ext)
    qcol = (iota(shape, 0) % sh.inner) // sh.up
    kcol = iota(shape, 1) // sh.up
    dx = kcol // sh.ey - qcol // sh.ay
    dy = kcol % sh.ey - qcol % sh.ay
    seen = (dx >= 0) & (dx <= 2) & (dy >= 0) & (dy <= 2)
    scores = nt(head_split(sh, queries), keys) * ((d // HEADS) ** -0.5)
    weights = jnp.exp(jnp.where(seen, scores, -1e30))
    weights = weights / jnp.sum(weights, axis=-1, keepdims=True)
    attended = head_join(sh, nn(weights, values))
    mid = take(tokens, sh.view(0, 0)) + nn(attended, wo[...])
    pre = nn(mid * inverse_rms(mid) * g2[...], wx[...])
    late = mid + nn(pre / (1.0 + jnp.exp(-pre)), wr[...])
    return nn(late, wd[...]), (tokens, queries, keys, values, weights, attended, mid, pre, late)


def backward(sh, ext, w, saved, cot, back_ref, emit):
    we, g1, wa, wo, g2, wx, wr, wd = w
    d = sh.width
    tokens, queries, keys, values, weights, attended, mid, pre, late = saved
    dclosed = TIME_STEP * cot
    emit("decode", tn(late, dclosed))
    dlate = nt(dclosed, wd[...])
    sig = 1.0 / (1.0 + jnp.exp(-pre))
    emit("reduce", tn(pre * sig, dlate))
    dpre = nt(dlate, wr[...]) * (sig * (1.0 + pre * (1.0 - sig)))
    r2 = inverse_rms(mid)
    unit = mid * r2
    emit("expand", tn(unit * g2[...], dpre))
    dn = nt(dpre, wx[...])
    emit("second", jnp.sum(dn * unit, axis=0, keepdims=True))
    y = dn * g2[...]
    dmid = dlate + r2 * (y - unit * jnp.mean(y * unit, axis=-1, keepdims=True))
    emit("output", tn(attended, dmid))
    dsplit = head_split(sh, nt(dmid, wo[...]))
    dweights = nt(dsplit, values)
    dvalues = tn(weights, dsplit)
    dscores = weights * (dweights - jnp.sum(dweights * weights, axis=-1, keepdims=True))
    dscores = dscores * ((d // HEADS) ** -0.5)
    dqueries = head_join(sh, nn(dscores, keys))
    dkeys = tn(dscores, head_split(sh, queries))
    r1 = inverse_rms(tokens)
    unit = tokens * r1
    normed = unit * g1[...]
    emit("query", tn(take(normed, sh.view(0, 0)), dqueries))
    emit("key", tn(normed, dkeys))
    emit("value", tn(normed, dvalues))
    dn = nt(dkeys, wa[:, d : 2 * d]) + nt(dvalues, wa[:, 2 * d :])
    dinner = nt(dqueries, wa[:, :d])
    back_ref[...] = dn
    at = 0
    for s, n in sh.view(0, 0):
        back_ref[s : s + n, :] += dinner[at : at + n]
        at += n
    dn = back_ref[...]
    emit("norm", jnp.sum(dn * unit, axis=0, keepdims=True))
    y = dn * g1[...]
    back_ref[...] = r1 * (y - unit * jnp.mean(y * unit, axis=-1, keepdims=True))
    at = 0
    for s, n in sh.view(0, 0):
        back_ref[s : s + n, :] += dmid[at : at + n]
        at += n
    dtokens = back_ref[...]
    emit("embed", tn(ext, dtokens))
    back_ref[...] = nt(dtokens, we[...])
    stencil_back(sh, ext, cot, back_ref)


class Packing:
    def __init__(self, sh, devices):
        d = sh.width
        sizes = [
            ("reduce", sh.hidden),
            ("expand", d * (sh.hidden // d)),
            ("decode", d),
            ("output", d),
            ("query", d),
            ("key", d),
            ("value", d),
            ("embed", sh.feat - sh.cube),
            ("small", 8),
        ]
        self.at, row = {}, 0
        for name, n in sizes:
            self.at[name] = (row, n)
            row += n
        unit = 8 * devices
        self.rows = -(-row // unit) * unit
        self.used = row
        self.unit = unit


SMALL = {"norm": 0, "second": 1, "misfit": 2, "energy": 3}


def make_emit(sh, pk, out_ref, prior):
    def emit(name, value):
        if name in SMALL:
            r = pk.at["small"][0] + SMALL[name]
            value = value if prior is None else value + prior[r : r + 1, :]
            out_ref[r : r + 1, :] = value
            return
        row, n = pk.at[name]
        if name == "embed":
            value = value[:n]
        pieces = [value]
        if name == "expand":
            pieces = [value[:, k : k + sh.width] for k in range(0, sh.hidden, sh.width)]
        for piece in pieces:
            m = piece.shape[0]
            add = piece if prior is None else piece + prior[row : row + m, :]
            out_ref[row : row + m, :] = add
            row += m

    return emit


def neighbour(counts, dx, dy):
    nx, ny = counts
    return (
        lax.rem(lax.axis_index("gx") + (dx + nx), nx),
        lax.rem(lax.axis_index("gy") + (dy + ny), ny),
    )


def greet(devices):
    barrier = pltpu.get_barrier_semaphore()
    for device in devices:
        pl.semaphore_signal(barrier, inc=1, device_id=device, device_id_type=MESH)
    pl.semaphore_wait(barrier, len(devices))


AROUND = [(dx, dy) for dx in (-1, 0, 1) for dy in (-1, 0, 1) if (dx, dy) != (0, 0)]


def spread(sh, counts, u, ext, send, recv):
    started = []
    for i, (dx, dy, src, dst, n) in enumerate(sh.copies()):
        copy = pltpu.make_async_remote_copy(
            src_ref=u.at[pl.ds(src, n)],
            dst_ref=ext.at[pl.ds(dst, n)],
            send_sem=send.at[i],
            recv_sem=recv.at[i],
            device_id=neighbour(counts, dx, dy),
            device_id_type=MESH,
        )
        copy.start()
        started.append(copy)
    at = 0
    for s, n in sh.view(0, 0):
        ext[s : s + n, :] = u[at : at + n, :]
        at += n
    for copy in started:
        copy.wait()


def exchange_orders(counts):
    nx, ny = counts
    bits = lambda n: [1 << k for k in range(n.bit_length() - 1)]
    ys = [("gy", s) for s in bits(ny)]
    xs = [("gx", s) for s in bits(nx)]
    head, y, x, z = ys[:1], ys[1:], xs[:1], xs[1:]
    return [head + y + x + z, head + x + z + y, head + z + y + x]


def partner(axis, s):
    gx, gy = lax.axis_index("gx"), lax.axis_index("gy")
    index = gx if axis == "gx" else gy
    bit = lax.rem(index // s, 2)
    other = index + s - 2 * s * bit
    return bit, ((other, gy) if axis == "gx" else (gx, other))


def start_gather(sh, counts, back, slots, send, recv):
    started = []
    place = 0
    for i, (dx, dy, dst, src, n) in enumerate(sh.copies()):
        copy = pltpu.make_async_remote_copy(
            src_ref=back.at[pl.ds(src, n)],
            dst_ref=slots.at[pl.ds(place, n)],
            send_sem=send.at[i],
            recv_sem=recv.at[i],
            device_id=neighbour(counts, -dx, -dy),
            device_id_type=MESH,
        )
        copy.start()
        started.append((copy, dst, place, n))
        place += n
    return started


def end_gather(sh, back, out, slots, started):
    at = 0
    for s, n in sh.view(0, 0):
        out[at : at + n, :] = back[s : s + n, :]
        at += n
    for copy, dst, place, n in started:
        copy.wait()
        out[dst : dst + n, :] += slots[place : place + n, :]


def steps_kernel(sh, pk, counts, parts, *refs):
    u0, goal, w, (out, cot0) = refs[0], refs[1], refs[2:10], refs[10:12]
    ext0, ext1, u1, back1, back0, cot1, packed, acc, slots, halo1, halo0 = refs[12:23]
    saved, wide, sems = refs[23:32], refs[32:36], refs[36:42]
    send, recv, spread_send, spread_recv, gather_send, gather_recv = sems
    for ref, value in zip(wide, (u0, goal, w[0], w[7])):
        ref[...] = jnp.zeros(ref.shape, F32)
        ref[: value.shape[0], : value.shape[1]] = value[...]
    u0, goal = wide[:2]
    w = (wide[2],) + tuple(w[1:7]) + (wide[3],)
    orders = exchange_orders(counts)
    greet([neighbour(counts, dx, dy) for dx, dy in AROUND] + [partner(*step)[1] for step in orders[0]])
    spread(sh, counts, u0, ext0, spread_send.at[0], spread_recv.at[0])
    closed, kept = forward(sh, ext0[...], w)
    u1[...] = stencil(sh, ext0[...], closed)
    for ref, value in zip(saved, kept):
        ref[...] = value
    spread(sh, counts, u1, ext1, spread_send.at[1], spread_recv.at[1])
    packed[pk.at["small"][0] :, :] = jnp.zeros((pk.rows - pk.at["small"][0], sh.width), F32)
    emit = make_emit(sh, pk, packed, None)
    closed, kept = forward(sh, ext1[...], w)
    residue = stencil(sh, ext1[...], closed) - goal[...]
    emit("misfit", jnp.sum(residue * residue, axis=0, keepdims=True))
    emit("energy", jnp.sum(goal[...] * goal[...], axis=0, keepdims=True))
    backward(sh, ext1[...], w, kept, 2.0 * residue, back1, emit)
    end_gather(sh, back1, cot1, halo1, start_gather(sh, counts, back1, halo1, gather_send.at[0], gather_recv.at[0]))
    steps = len(orders[0])
    where = []
    base = 0
    for order, start, rows in parts:
        where.append((start, rows, base))
        base += rows
    history = [[] for _ in parts]

    def halve(p, k):
        start, rows, base = where[p]
        bit, device = partner(*orders[parts[p][0]][k])
        half = rows // 2
        keep = pl.multiple_of(start + bit * half, 8)
        give = pl.multiple_of(start + half - bit * half, 8)
        source = packed if k == 0 else acc
        copy = pltpu.make_async_remote_copy(
            src_ref=source.at[pl.ds(give, half)],
            dst_ref=slots.at[pl.ds(base, half)],
            send_sem=send.at[p, k],
            recv_sem=recv.at[p, k],
            device_id=device,
            device_id_type=MESH,
        )
        copy.start()
        history[p].append((keep, half, device))
        return copy, source, keep, half, base

    def add(p, k, flight):
        copy, source, keep, half, base = flight
        copy.wait()
        target = acc if k < steps - 1 else out
        target[pl.ds(keep, half), :] = source[pl.ds(keep, half), :] + slots[pl.ds(base, half), :]
        where[p] = (keep, half, base + half)

    def collect(p, k):
        keep, half, device = history[p][k]
        copy = pltpu.make_async_remote_copy(
            src_ref=out.at[pl.ds(keep, half)],
            dst_ref=out.at[pl.ds(keep, half)],
            send_sem=send.at[p, steps + k],
            recv_sem=recv.at[p, steps + k],
            device_id=device,
            device_id_type=MESH,
        )
        copy.start()
        return copy

    every = range(len(parts))
    first = pk.at["query"][0]
    early = [p for p in every if parts[p][1] + parts[p][2] <= first]
    flights = {}
    emit = make_emit(sh, pk, packed, packed)

    def emit_and_send(name, value):
        emit(name, value)
        if name == "output":
            for p in early:
                flights[p] = halve(p, 0)
        if name == "query":
            for p in early:
                add(p, 0, flights[p])
                flights[p] = halve(p, 1)

    backward(sh, ext0[...], w, tuple(ref[...] for ref in saved), cot1[...], back0, emit_and_send)
    halos = start_gather(sh, counts, back0, halo0, gather_send.at[1], gather_recv.at[1])
    for p in every:
        if p not in early:
            flights[p] = halve(p, 0)
    end_gather(sh, back0, cot0, halo0, halos)
    for k in range(steps):
        for p in every:
            if k == 0 and p in early:
                continue
            add(p, k, flights[p])
            flights[p] = halve(p, k + 1) if k < steps - 1 else collect(p, k)
    for k in reversed(range(steps)):
        for p in every:
            flights[p].wait()
            if k > 0:
                flights[p] = collect(p, k - 1)


def finish_kernel(sh, pk, entries, packed, cot, loss, field, embed, norm, attend, output, second, expand, reduce, decode):
    small = pk.at["small"][0]
    energy = jnp.sum(packed[small + SMALL["energy"] : small + SMALL["energy"] + 1, :], axis=1, keepdims=True)
    misfit = jnp.sum(packed[small + SMALL["misfit"] : small + SMALL["misfit"] + 1, :], axis=1, keepdims=True)
    scale = entries / energy
    loss[...] = misfit / energy
    field[...] = scale * cot[...]
    norm[...] = scale * packed[small : small + 1, :]
    second[...] = scale * packed[small + 1 : small + 2, :]

    def piece(name):
        row, n = pk.at[name]
        return scale * packed[row : row + n, :]

    embed[...] = piece("embed")
    output[...] = piece("output")
    reduce[...] = piece("reduce")
    decode[...] = piece("decode")[:, : decode.shape[1]]
    d = sh.width
    for k, name in enumerate(("query", "key", "value")):
        attend[:, k * d : (k + 1) * d] = piece(name)
    row = pk.at["expand"][0]
    for k in range(sh.hidden // d):
        expand[:, k * d : (k + 1) * d] = scale * packed[row + k * d : row + (k + 1) * d, :]


def call(kernel, outs, args, scratch=(), collective=None):
    vm = pl.BlockSpec(memory_space=pltpu.VMEM)
    extra = {} if collective is None else dict(collective_id=collective, has_side_effects=True)
    return pl.pallas_call(
        kernel,
        out_shape=[jax.ShapeDtypeStruct(s, F32) for s in outs],
        in_specs=[vm] * len(args),
        out_specs=[vm] * len(outs),
        scratch_shapes=list(scratch),
        compiler_params=pltpu.CompilerParams(vmem_limit_bytes=VMEM_LIMIT, **extra),
    )(*args)


def to_tokens(sh, block):
    x = block.reshape(sh.ax, PATCH, sh.ay, PATCH, 3, sh.up, PATCH).transpose(0, 2, 5, 4, 1, 3, 6)
    return x.reshape(sh.inner, 3 * sh.cube)


def from_tokens(sh, tokens, shape):
    x = tokens[:, : 3 * sh.cube].reshape(sh.ax, sh.ay, sh.up, 3, PATCH, PATCH, PATCH)
    return x.transpose(0, 4, 1, 5, 3, 2, 6).reshape(shape)


def shards(counts, field, target, embed_weight, norm_gain, attend_weight, output_weight, second_gain, expand_weight, reduce_weight, decode_weight):
    width, hidden = expand_weight.shape
    sh = Shape(field.shape, width, hidden)
    devices = counts[0] * counts[1]
    pk = Packing(sh, devices)
    blocks = pk.rows // pk.unit
    cuts = [blocks * share // 10 for share in (0, 3, 5, 6, 8, 9, 10)]
    spans = zip((0, 1, 2, 0, 1, 2), cuts, cuts[1:])
    parts = [(order, a * pk.unit, (b - a) * pk.unit) for order, a, b in spans if b > a]
    weights = (
        embed_weight,
        norm_gain.reshape(1, width),
        attend_weight,
        output_weight,
        second_gain.reshape(1, width),
        expand_weight,
        reduce_weight,
        decode_weight,
    )
    ext_shape, inner_shape = (sh.ext, sh.feat), (sh.inner, sh.feat)
    slabs = sh.copies()
    sems = [pltpu.SemaphoreType.DMA((2, len(slabs)))] * 4
    slot_rows = sum(n[4] for n in slabs)
    tokens_shape, query_shape = (sh.ext, width), (sh.inner, width)
    saved_shapes = [
        tokens_shape,
        query_shape,
        tokens_shape,
        tokens_shape,
        (HEADS * sh.inner, sh.ext),
        query_shape,
        query_shape,
        (sh.inner, hidden),
        query_shape,
    ]
    goal = to_tokens(sh, target)
    packed_shape = (pk.rows, width)
    steps = len(exchange_orders(counts)[0])
    halo_shape = (slot_rows, sh.feat)
    scratch = [ext_shape, ext_shape, inner_shape, ext_shape, ext_shape, inner_shape] + [packed_shape] * 3
    scratch += [halo_shape] * 2 + saved_shapes
    scratch += [inner_shape, inner_shape, (sh.feat, width), (width, sh.feat)]
    summed, cot = call(
        functools.partial(steps_kernel, sh, pk, counts, parts),
        [packed_shape, inner_shape],
        (to_tokens(sh, field), goal) + weights,
        [pltpu.VMEM(shape, F32) for shape in scratch]
        + [pltpu.SemaphoreType.DMA((len(parts), 2 * steps))] * 2
        + sems,
        1,
    )
    entries = float(np.prod(field.shape) * devices)
    params = (embed_weight, norm_gain, attend_weight, output_weight, second_gain, expand_weight, reduce_weight, decode_weight)
    outs = [(1, 1), inner_shape] + [p.shape if p.ndim == 2 else (1, width) for p in params]
    done = call(functools.partial(finish_kernel, sh, pk, entries), outs, (summed, cot))
    grads = tuple(g.reshape(p.shape) for g, p in zip(done[2:], params))
    return (done[0].reshape(()), from_tokens(sh, done[1], field.shape)) + grads


def solution(mesh):
    counts = (mesh.shape["gx"], mesh.shape["gy"])
    in_specs = (P("gx", "gy", None), P("gx", "gy", None), P(), P(), P(), P(), P(), P(), P(), P())
    out_specs = (P(), P("gx", "gy", None), P(), P(), P(), P(), P(), P(), P(), P())
    return jax.shard_map(
        functools.partial(shards, counts), mesh=mesh, in_specs=in_specs, out_specs=out_specs, check_vma=False
    )
```
